32 devices in a mesh: parts: 2 (over x), sec: 16 (over z, y, core).
Axes of the slice: x: 2, y: 2, z: 4, core: 2. Of those that a mesh axis runs over, the one named last changes fastest.
Arguments:
- psi: bfloat16 [256, 4096], P(('parts', 'sec')), parts along dimension 0, may hold values from -6 to 6
- left_env: bfloat16 [128, 26, 4096], P(('parts', 'sec')), parts along dimension 0, may hold values from -0.75 to 0.75
- right_env: bfloat16 [128, 26, 4096], P(('parts', 'sec')), parts along dimension 0, may hold values from -0.75 to 0.75
- couple: float32 [256, 2, 26], P(('parts', 'sec')), parts along dimension 0, may hold values from -1.25 to 1.25
- left_sector: int32 [256], P(('parts', 'sec')), parts along dimension 0, may hold values from 0 to 3
- right_owner: int32 [256, 1], P(('parts', 'sec')), parts along dimension 0, may hold values from 0 to 15; in each aligned block of 8 rows (0 to 7, 8 to 15, ...) at most 2 rows name the same one
- right_local: int32 [256], P(('parts', 'sec')), parts along dimension 0, may hold values from 0 to 3
- channel: int32 [256, 2], P(('parts', 'sec')), parts along dimension 0, may hold values from 0 to 25
Outputs:
- second: float32 [256, 4096], P(('parts', 'sec')), parts along dimension 0
- direction: bfloat16 [256, 4096], P(('parts', 'sec')), parts along dimension 0
- projected: float32 [6], P('parts'), parts along dimension 0
The draws below stay inside these ranges and needn't reach their ends.
There are 2 independent parts, one for each index of `parts`. The reference program is written for one: setup_inputs(seed, part) draws one part's arguments, and reference() takes and returns one part's arrays. A program takes and returns all parts, laid end to end along the dimension named above; each array names one. Nothing has to cross between parts.
Inputs may be any that keep to these rules, and one draw needn't show every extreme that they name: `right_owner`: among the 8 blocks of one device at most 2 have the same right owner.
All inputs are finite; a program needn't handle non-finite values.
Results may differ from the reference program's by a relative error of at most 0.001.
The reference program's roundings to bfloat16 on the way (of `psi`, `lcomb`, `rsel`, `image` and `zed`) count: a program that leaves them out, or rounds other values in their place, can miss the bound.
Values may be sent and summed in bfloat16 or wider, within the bound.
No kernel may reach another device: no remote copies, remote signals or barrier semaphores. Data moves between devices by JAX's collectives and lax.ppermute only.
A program may use at most 128 MiB of HBM per device.

```python
import math
import jax
import jax.numpy as jnp
import numpy as np
from jax import lax

B = 64
W = 26
K = 2
CAP = 2
LS_DEV = 4
RS_DEV = 4
BLK_DEV = 8
NBLK = 128
NL = 64
NR = 64
N_SEC = 16


def set_ends(values, own_key, smallest, largest):
    spot = [jax.random.randint(jax.random.fold_in(own_key, axis), (), 0, length) for axis, length in enumerate(values.shape)]
    main_axis = values.shape.index(max(values.shape))
    next_to = spot[:main_axis] + [(spot[main_axis] + 1) % values.shape[main_axis]] + spot[main_axis + 1:]
    return values.at[tuple(spot)].set(smallest).at[tuple(next_to)].set(largest)


def steps_of(stream_key, extent, split, smallest, top_value):
    level = 1.0
    for dim, shards_of in split:
        heights = jax.random.uniform(jax.random.fold_in(jax.random.fold_in(stream_key, 6), dim), (shards_of,), jnp.float32, smallest / len(split), top_value / len(split))
        level = level * jnp.repeat(jnp.exp(heights), extent[dim] // shards_of).reshape((-1,) + (1,) * (len(extent) - 1 - dim))
    return level


def routed_block(own_key, own, number, rows, amount, top, most, lean):
    sequence = jax.random.permutation(own_key, amount)
    crowded, common = shares(amount, rows * top, most, lean, True), shares(amount, rows * top, most, lean, False)
    places = jnp.arange(amount)

    def named(lengths, rotation):
        used = int((lengths > 0).sum())
        fixed = max(1, used // 4)
        passed = fixed + (places - fixed + rotation * (used - fixed)) % max(1, amount - fixed)
        return jnp.zeros((amount,), jnp.int32).at[sequence[jnp.where(places < fixed, places, passed)]].set(jnp.asarray(lengths, jnp.int32))

    lengths = jnp.where(number % 4 == 0, named(crowded, number // 4), named(common, number - number // 4 - 1))
    mixed = jax.random.permutation(jax.random.fold_in(own, 3), amount)
    donor, sink = mixed[0:amount // 2 * 2:2], mixed[1:amount // 2 * 2:2]
    margin = jnp.minimum(lengths[donor] - 1, most - lengths[sink]) // 2
    margin = jnp.where((donor == sequence[0]) | (sink == sequence[0]) | (lengths[sink] == 0), 0, jnp.maximum(margin, 0))
    passed = jax.random.randint(jax.random.fold_in(own, 4), (amount // 2,), 0, 1 << 20) % (margin + 1)
    lengths = lengths.at[donor].add(-passed).at[sink].add(passed)
    items = jnp.searchsorted(jnp.cumsum(lengths), jnp.arange(rows * top), side="right").astype(jnp.int32)
    listing = items.reshape(top, rows).T
    listing = listing[jax.random.permutation(jax.random.fold_in(own, 1), rows)]
    rotation = jax.random.randint(jax.random.fold_in(own, 2), (rows, 1), 0, top)
    return jnp.take_along_axis(listing, (jnp.arange(top)[None, :] + rotation) % top, axis=1)


def shares(amount, total, limit, skew, full):
    portions = [(1 << 20) // math.isqrt(standing ** skew) + 1 for standing in range(1, amount + 1)]
    largest = limit if full else min(limit, max(-(-total // amount), total * portions[0] // sum(portions)))
    least = 1 if total - largest >= amount - 1 else 0
    counts, rest = [largest] + [least] * (amount - 1), total - largest - least * (amount - 1)
    while rest > 0:
        candidates = [i for i in range(1, amount) if counts[i] < largest] or [i for i in range(1, amount) if counts[i] < limit]
        whole, budget = sum([portions[i] for i in candidates]), rest
        for i in candidates:
            addition = min(limit - counts[i], max(1, budget * portions[i] // whole), rest)
            counts[i] = counts[i] + addition
            rest = rest - addition
    return np.array(counts)


def scatter_about(stream_key, shape, spread, bound, shards=(), kind=jnp.bfloat16):
    array = spread * jax.random.normal(stream_key, shape, jnp.float32)
    if shards:
        array = array * steps_of(stream_key, shape, shards, -0.22, 0.18)
    return jnp.clip(array, -bound, bound).astype(kind)


def setup_inputs(seed: int = 0, part: int = 0) -> dict:
    splits = jax.random.split(jax.random.key(seed), 9)
    own_keys = jax.random.split(jax.random.fold_in(splits[8], part), 9)
    psi = scatter_about(own_keys[0], (NBLK, B * B), 1.0, 6.0, ((0, 16),))
    left_env = scatter_about(own_keys[1], (NL, W, B * B), B ** -0.5, 0.75, ((0, 16),))
    right_env = scatter_about(own_keys[2], (NR, W, B * B), B ** -0.5, 0.75, ((0, 16),))
    couple = scatter_about(own_keys[3], (NBLK, K, W), W ** -0.5, 1.25, ((0, 16),), jnp.float32)
    left_sector = set_ends(jax.random.randint(own_keys[4], (NBLK,), 0, LS_DEV), jax.random.fold_in(own_keys[4], 1), 0, LS_DEV - 1).astype(jnp.int32)
    right_owner_keys = jax.random.split(jax.random.fold_in(own_keys[5], 1), NBLK // BLK_DEV)
    right_owner_turns = jax.random.permutation(jax.random.fold_in(own_keys[5], 3), NBLK // BLK_DEV)
    right_owner = jax.vmap(lambda own, number: routed_block(jax.random.fold_in(own_keys[5], 2), own, number, BLK_DEV, N_SEC, 1, CAP, 2))(right_owner_keys, right_owner_turns).reshape((NBLK, 1))
    right_local = set_ends(jax.random.randint(own_keys[6], (NBLK,), 0, RS_DEV), jax.random.fold_in(own_keys[6], 1), 0, RS_DEV - 1).astype(jnp.int32)
    channel = set_ends(jax.random.randint(own_keys[7], (NBLK, K), 0, W), jax.random.fold_in(own_keys[7], 1), 0, W - 1).astype(jnp.int32)
    return dict(psi=psi, left_env=left_env, right_env=right_env, couple=couple, left_sector=left_sector, right_owner=right_owner, right_local=right_local, channel=channel)


def left_part(left_env, couple, lglob, k):
    lenv = left_env[lglob[k]].astype(jnp.float32)
    return jnp.einsum('jw,wab->jab', couple[k], lenv, precision=lax.Precision.HIGHEST).astype(jnp.bfloat16)

def reference(psi, left_env, right_env, couple, left_sector, right_owner, right_local, channel):
    psi = psi.reshape(psi.shape[0], B, B)
    left_env = left_env.reshape(left_env.shape[0], W, B, B)
    right_env = right_env.reshape(right_env.shape[0], W, B, B)
    blocks = psi.shape[0]
    order = jnp.arange(blocks, dtype=jnp.int32)
    lglob = (order // BLK_DEV).astype(jnp.int32) * LS_DEV + left_sector
    rglob = right_owner[:, 0] * RS_DEV + right_local

    def first(k):
        lcomb = left_part(left_env, couple, lglob, k)
        rsel = right_env[rglob[k]][channel[k]].astype(jnp.float32)
        image = jnp.einsum('jab,bc->jac', lcomb.astype(jnp.float32), psi[k].astype(jnp.float32)).astype(jnp.bfloat16)
        return jnp.einsum('jab,jbc->ac', image.astype(jnp.float32), rsel)
    hpsi = lax.map(first, order, batch_size=256)
    base = psi.astype(jnp.float32)
    theta = jnp.sum(base * hpsi) / jnp.sum(base * base)
    resid = hpsi - theta * base
    rr = jnp.sum(resid * resid)
    count = NBLK * B * B
    direction = (resid / jnp.sqrt(rr / count + 1e-06)).astype(jnp.bfloat16)

    def again(k):
        lcomb = left_part(left_env, couple, lglob, k)
        rsel = right_env[rglob[k]][channel[k]].astype(jnp.float32)
        zed = jnp.einsum('ab,jbc->jac', direction[k].astype(jnp.float32), rsel).astype(jnp.bfloat16)
        return jnp.einsum('jab,jbc->ac', lcomb.astype(jnp.float32), zed.astype(jnp.float32))
    second = lax.map(again, order, batch_size=256)
    dirf = direction.astype(jnp.float32)
    closing = jnp.sum(dirf * second) / jnp.sum(dirf * dirf)
    projected = jnp.stack([theta, jnp.sqrt(rr / count), closing]).astype(jnp.float32)
    return (second.reshape(blocks, B * B), direction.reshape(blocks, B * B), projected)
```

```python
import functools

import jax
import jax.numpy as jnp
from jax import lax
from jax.experimental import pallas as pl
from jax.experimental.pallas import tpu as pltpu
from jax.sharding import PartitionSpec as P

B = 64
CAP = 2
LANES = 128
STATS = 8
TINY = 1e-30
F32 = jnp.float32
BF16 = jnp.bfloat16


def rounded_up(value, step):
    return -(-value // step) * step


def each(count, body):
    if count <= 8:
        for i in range(count):
            body(i)
    else:
        pl.loop(0, count)(body)


def dot(a, b):
    return jnp.dot(a, b, preferred_element_type=F32)


def unroll_rows(read, stage, groups):
    def group(g):
        for t in range(B * B // LANES):
            tile = read(g, t)
            base = g * (8 * B) + 2 * t
            stage[pl.ds(base, 8, stride=B), :] = tile
            stage[pl.ds(base + 1, 8, stride=B), :] = pltpu.roll(tile, B, 1)

    each(groups, group)


def request_kernel(chans, owner, local, channel, table, slot, seen):
    blocks, terms = channel.shape

    @pl.loop(0, seen.shape[0])
    def _(p):
        seen[p] = 0

    @pl.loop(0, table.shape[0])
    def _(i):
        table[i] = 0

    def block(k):
        own = owner[k, 0]
        rank = seen[own]
        seen[own] = rank + 1
        slot[k] = own * CAP + rank
        for j in range(terms):
            table[(own * CAP + rank) * terms + j] = local[k] * chans + channel[k, j]

    each(blocks, block)


def right_kernel(env, out, stage):
    chans = env.shape[1]
    low = lax.broadcasted_iota(jnp.int32, (8, LANES), 1) < B
    rows = env[0].astype(F32)
    for g in range(-(-chans // 8)):
        height = min(8, chans - 8 * g)
        for t in range(B * B // LANES):
            tile = rows[8 * g : 8 * g + height, t * LANES : (t + 1) * LANES]
            turned = pltpu.roll(tile, B, 1)
            base = 8 * g * B + 2 * t
            stage[pl.ds(base, height, stride=B), :] = jnp.where(low[:height], tile, turned)
            stage[pl.ds(base + 1, height, stride=B), :] = jnp.where(low[:height], turned, tile)
    out[...] = stage[...].reshape(out.shape).astype(BF16)


def left_kernel(sector, couple, env, psi, lcomb, image, wave, weights, envs, stage, wave_stage):
    blocks, terms, chans = couple.shape
    lsecs = env.shape[0]
    wide = envs.shape[0]
    pitch = wide // lsecs
    rows = blocks * terms
    weights[...] = jnp.zeros_like(weights)
    envs[...] = jnp.zeros_like(envs)
    for s in range(lsecs):
        envs[s * pitch : s * pitch + chans, :] = env[s]

    def weigh(k):
        weights[pl.ds(k * terms, terms), 0:chans] = couple[k]

    each(blocks, weigh)

    def turn(k):
        place = pl.ds(k * terms, terms)
        weights[place, :] = pltpu.roll(weights[place, :], sector[k] * pitch, 1)

    each(blocks, turn)
    exact = weights[...]
    high = exact.astype(BF16)
    rest = exact - high.astype(F32)
    middle = rest.astype(BF16)
    low = (rest - middle.astype(F32)).astype(BF16)
    parts = jnp.concatenate([high, middle, low], axis=0)
    width = 512
    for n in range(B * B // width):
        sums = dot(parts, envs[:, n * width : (n + 1) * width])
        total = sums[:rows] + (sums[rows : 2 * rows] + sums[2 * rows :])
        for g in range(rows // 8):
            for t in range(width // LANES):
                tile = total[8 * g : 8 * g + 8, t * LANES : (t + 1) * LANES]
                base = 8 * g * B + 2 * (n * (width // LANES) + t)
                stage[pl.ds(base, 8, stride=B), :] = tile
                stage[pl.ds(base + 1, 8, stride=B), :] = pltpu.roll(tile, B, 1)

    def waves(g):
        held = psi[pl.ds(pl.multiple_of(8 * g, 8), 8), :].astype(F32)
        for t in range(B * B // LANES):
            tile = held[:, t * LANES : (t + 1) * LANES]
            base = 8 * g * B + 2 * t
            wave_stage[pl.ds(base, 8, stride=B), :] = tile
            wave_stage[pl.ds(base + 1, 8, stride=B), :] = pltpu.roll(tile, B, 1)

    each(blocks // 8, waves)

    def block(k):
        left = stage[pl.ds(pl.multiple_of(k * (terms * B), terms * B), terms * B), 0:B].astype(BF16)
        base = wave_stage[pl.ds(pl.multiple_of(k * B, B), B), 0:B]
        lcomb[k] = left
        wave[k] = base
        image[k] = dot(left, base.astype(BF16)).astype(BF16)

    each(blocks, block)


def gather_kernel(table, env, out):
    terms = 2

    def fill(i):
        for j in range(terms):
            out[i, :, j * B : (j + 1) * B] = env[table[i * terms + j]][:, j * B : (j + 1) * B]

    each(out.shape[0], fill)


def closed(products):
    return products[:B, :B] + pltpu.roll(products[B:, :], B, 1)[:, :B]


def image_kernel(slot, received, lcomb, image, wave, hpsi, rsel, stats, part):
    blocks = lcomb.shape[0]
    lanes = stats.shape[2]
    lane = lax.broadcasted_iota(jnp.int32, (1, lanes), 1)
    part[...] = jnp.zeros_like(part)

    def total(values):
        return jnp.sum(jnp.sum(values, axis=0, keepdims=True), axis=1, keepdims=True)

    def block(k):
        right = received[slot[k]]
        rsel[k] = right
        base = wave[k]
        h = closed(dot(image[k], right))
        hpsi[k] = h
        norm = total(base * base)
        cross = total(base * h)
        resid = h - cross / jnp.maximum(norm, TINY) * base
        zed = dot(resid.astype(BF16), right).astype(BF16)
        applied = closed(dot(lcomb[k], zed))
        sums = (
            norm,
            cross,
            total(resid * resid),
            total(resid * base),
            total(resid * applied),
            total(base * applied),
            total(resid * h),
        )
        here = lane == k
        for i, value in enumerate(sums):
            part[i : i + 1, :] = jnp.where(here, value, part[i : i + 1, :])

    each(blocks, block)
    whole = part[...]

    def spread(p):
        stats[p] = whole

    each(stats.shape[0], spread)


def second_kernel(count, stats, hpsi, wave, rsel, lcomb, second, direction, projected, stage, dir_stage):
    blocks = lcomb.shape[0]
    norm, cross, square, mixed, applied, crossed, image = (stats[:, i, :] for i in range(7))

    def total(values):
        return jnp.sum(jnp.sum(values, axis=0, keepdims=True), axis=1, keepdims=True)

    theta = total(cross) / total(norm)
    shift = theta - cross / jnp.maximum(norm, TINY)
    rr = total(square - 2.0 * shift * mixed + shift * shift * norm)
    along = total(applied - shift * (image + crossed) + shift * shift * cross)
    spread = rr / count
    projected[0] = theta[0, 0]
    projected[1] = jnp.sqrt(spread)[0, 0]
    projected[2] = (along / rr)[0, 0]
    scale = 1.0 / jnp.sqrt(spread + 1e-06)

    def block(k):
        place = pl.ds(pl.multiple_of(k * B, B), B)
        step = ((hpsi[k] - theta * wave[k]) * scale).astype(BF16)
        dir_stage[place, 0:B] = step.astype(F32)
        zed = dot(step, rsel[k]).astype(BF16)
        stage[place, 0:B] = closed(dot(lcomb[k], zed))

    each(blocks, block)
    low = lax.broadcasted_iota(jnp.int32, (8, LANES), 1) < B

    def rows(g):
        place = pl.ds(pl.multiple_of(8 * g, 8), 8)
        for t in range(B * B // LANES):
            base = 8 * g * B + 2 * t
            lanes = slice(t * LANES, (t + 1) * LANES)
            for source, target in ((stage, second), (dir_stage, direction)):
                even = source[pl.ds(base, 8, stride=B), :]
                odd = source[pl.ds(base + 1, 8, stride=B), :]
                target[place, lanes] = jnp.where(low, even, pltpu.roll(odd, B, 1)).astype(target.dtype)

    each(blocks // 8, rows)


VMEM = pl.BlockSpec(memory_space=pltpu.VMEM)
SMEM = pl.BlockSpec(memory_space=pltpu.SMEM)


def params(mib=40):
    return pltpu.CompilerParams(vmem_limit_bytes=mib << 20)


def per_device(psi, left_env, right_env, couple, left_sector, right_owner, right_local, channel):
    peers = lax.axis_size("sec")
    blocks = psi.shape[0]
    _, terms, chans = couple.shape
    lsecs = left_env.shape[0]
    rsecs = right_env.shape[0]
    slots = peers * CAP
    lanes = rounded_up(blocks, LANES)
    of = jax.ShapeDtypeStruct

    def exchange(values):
        return lax.all_to_all(values, "sec", split_axis=0, concat_axis=0, tiled=True)

    table, slot = pl.pallas_call(
        functools.partial(request_kernel, chans),
        out_shape=(of((slots * terms,), jnp.int32), of((blocks,), jnp.int32)),
        in_specs=[SMEM] * 3,
        out_specs=(SMEM, SMEM),
        scratch_shapes=[pltpu.SMEM((peers,), jnp.int32)],
        name="request",
    )(right_owner, right_local, channel)
    wanted = exchange(table.reshape(peers, CAP * terms)).reshape(slots * terms)

    right = pl.pallas_call(
        right_kernel,
        grid=(rsecs,),
        out_shape=of((rsecs * chans, B, LANES), BF16),
        in_specs=[pl.BlockSpec((1, chans, B * B), lambda s: (s, 0, 0))],
        out_specs=pl.BlockSpec((chans, B, LANES), lambda s: (s, 0, 0)),
        scratch_shapes=[pltpu.VMEM((chans * B, LANES), F32)],
        compiler_params=params(),
        cost_estimate=pl.CostEstimate(flops=10_000_000, bytes_accessed=3_000_000, transcendentals=0),
        name="right",
    )(right_env)

    wide = rounded_up(lsecs * rounded_up(chans, 32), LANES)
    lcomb, image, wave = pl.pallas_call(
        left_kernel,
        out_shape=(
            of((blocks, terms * B, B), BF16),
            of((blocks, terms * B, B), BF16),
            of((blocks, B, B), F32),
        ),
        in_specs=[SMEM, VMEM, VMEM, VMEM],
        out_specs=(VMEM, VMEM, VMEM),
        scratch_shapes=[
            pltpu.VMEM((blocks * terms, wide), F32),
            pltpu.VMEM((wide, B * B), BF16),
            pltpu.VMEM((blocks * terms * B, LANES), F32),
            pltpu.VMEM((blocks * B, LANES), F32),
        ],
        compiler_params=params(),
        cost_estimate=pl.CostEstimate(flops=100_000_000, bytes_accessed=3_000_000, transcendentals=0),
        name="left",
    )(left_sector, couple, left_env, psi)

    sent = pl.pallas_call(
        gather_kernel,
        out_shape=of((slots, B, LANES), BF16),
        in_specs=[SMEM, VMEM],
        out_specs=VMEM,
        compiler_params=params(),
        name="gather",
    )(wanted, right)
    received = exchange(sent.reshape(peers, CAP * B, LANES)).reshape(slots, B, LANES)

    hpsi, rsel, stats = pl.pallas_call(
        image_kernel,
        out_shape=(
            of((blocks, B, B), F32),
            of((blocks, B, LANES), BF16),
            of((peers, STATS, lanes), F32),
        ),
        in_specs=[SMEM] + [VMEM] * 4,
        out_specs=(VMEM, VMEM, VMEM),
        scratch_shapes=[pltpu.VMEM((STATS, lanes), F32)],
        compiler_params=params(),
        name="image",
    )(slot, received, lcomb, image, wave)
    stats = exchange(stats)

    second, direction, projected = pl.pallas_call(
        functools.partial(second_kernel, float(blocks * peers * B * B)),
        out_shape=(of((blocks, B * B), F32), of((blocks, B * B), BF16), of((3,), F32)),
        in_specs=[VMEM] * 5,
        out_specs=(VMEM, VMEM, SMEM),
        scratch_shapes=[
            pltpu.VMEM((blocks * B, LANES), F32),
            pltpu.VMEM((blocks * B, LANES), F32),
        ],
        compiler_params=params(),
        name="second",
    )(stats, hpsi, wave, rsel, lcomb)
    return second, direction, projected


def solution(mesh):
    placed = (
        P(("parts", "sec"), None),
        P(("parts", "sec"), None, None),
        P(("parts", "sec"), None, None),
        P(("parts", "sec"), None, None),
        P(("parts", "sec")),
        P(("parts", "sec"), None),
        P(("parts", "sec")),
        P(("parts", "sec"), None),
    )
    return jax.shard_map(
        per_device,
        mesh=mesh,
        in_specs=placed,
        out_specs=(P(("parts", "sec"), None), P(("parts", "sec"), None), P("parts")),
        check_vma=False,
    )
```

```python
import functools

import jax
import jax.numpy as jnp
from jax import lax
from jax.experimental import pallas as pl
from jax.experimental.pallas import tpu as pltpu
from jax.sharding import PartitionSpec as P

B = 64
CAP = 2
LANES = 128
STATS = 8
TINY = 1e-30
F32 = jnp.float32
BF16 = jnp.bfloat16


def rounded_up(value, step):
    return -(-value // step) * step


def each(count, body):
    if count <= 32:
        for i in range(count):
            body(i)
    else:
        pl.loop(0, count)(body)


def dot(a, b):
    return jnp.dot(a, b, preferred_element_type=F32)


def unroll_rows(read, stage, groups):
    def group(g):
        for t in range(B * B // LANES):
            tile = read(g, t)
            base = g * (8 * B) + 2 * t
            stage[pl.ds(base, 8, stride=B), :] = tile
            stage[pl.ds(base + 1, 8, stride=B), :] = pltpu.roll(tile, B, 1)

    each(groups, group)


def request_kernel(chans, owner, local, channel, table, slot, seen):
    terms, blocks = channel.shape

    def clear(p):
        seen[p] = 0
        for i in range(table.shape[2]):
            table[p, 0, i] = 0

    each(seen.shape[0], clear)

    def block(k):
        own = owner[0, k]
        rank = seen[own]
        seen[own] = rank + 1
        slot[k] = own * CAP + rank
        for j in range(terms):
            table[own, 0, rank * terms + j] = local[k] * chans + channel[j, k]

    each(blocks, block)


def right_kernel(env, out, stage):
    chans = env.shape[1]
    low = lax.broadcasted_iota(jnp.int32, (8, LANES), 1) < B
    rows = env[0].astype(F32)
    for g in range(-(-chans // 8)):
        height = min(8, chans - 8 * g)
        for t in range(B * B // LANES):
            tile = rows[8 * g : 8 * g + height, t * LANES : (t + 1) * LANES]
            turned = pltpu.roll(tile, B, 1)
            base = 8 * g * B + 2 * t
            stage[pl.ds(base, height, stride=B), :] = jnp.where(low[:height], tile, turned)
            stage[pl.ds(base + 1, height, stride=B), :] = jnp.where(low[:height], turned, tile)
    out[...] = stage[...].reshape(out.shape).astype(BF16)


def left_kernel(sector, couple, env, psi, lcomb, image, wave, weights, envs, stage, wave_stage):
    blocks, terms, chans = couple.shape
    lsecs = env.shape[0]
    wide = envs.shape[0]
    pitch = wide // lsecs
    rows = blocks * terms
    weights[...] = jnp.zeros_like(weights)
    envs[...] = jnp.zeros_like(envs)
    for s in range(lsecs):
        envs[s * pitch : s * pitch + chans, :] = env[s]

    def weigh(k):
        weights[pl.ds(k * terms, terms), 0:chans] = couple[k]

    each(blocks, weigh)

    def turn(k):
        place = pl.ds(k * terms, terms)
        weights[place, :] = pltpu.roll(weights[place, :], sector[k] * pitch, 1)

    each(blocks, turn)
    exact = weights[...]
    high = exact.astype(BF16)
    rest = exact - high.astype(F32)
    middle = rest.astype(BF16)
    low = (rest - middle.astype(F32)).astype(BF16)
    parts = jnp.concatenate([high, middle, low], axis=0)
    width = 512
    for n in range(B * B // width):
        sums = dot(parts, envs[:, n * width : (n + 1) * width])
        total = sums[:rows] + (sums[rows : 2 * rows] + sums[2 * rows :])
        for g in range(rows // 8):
            for t in range(width // LANES):
                tile = total[8 * g : 8 * g + 8, t * LANES : (t + 1) * LANES]
                base = 8 * g * B + 2 * (n * (width // LANES) + t)
                stage[pl.ds(base, 8, stride=B), :] = tile
                stage[pl.ds(base + 1, 8, stride=B), :] = pltpu.roll(tile, B, 1)

    def waves(g):
        held = psi[pl.ds(pl.multiple_of(8 * g, 8), 8), :].astype(F32)
        for t in range(B * B // LANES):
            tile = held[:, t * LANES : (t + 1) * LANES]
            base = 8 * g * B + 2 * t
            wave_stage[pl.ds(base, 8, stride=B), :] = tile
            wave_stage[pl.ds(base + 1, 8, stride=B), :] = pltpu.roll(tile, B, 1)

    each(blocks // 8, waves)

    def block(k):
        left = stage[pl.ds(pl.multiple_of(k * (terms * B), terms * B), terms * B), 0:B].astype(BF16)
        base = wave_stage[pl.ds(pl.multiple_of(k * B, B), B), 0:B]
        lcomb[k] = left
        wave[k] = base
        image[k] = dot(left, base.astype(BF16)).astype(BF16)

    each(blocks, block)


def gather_kernel(table, env, out):
    terms = LANES // B

    def fill(p):
        for c in range(CAP):
            for j in range(terms):
                half = slice(j * B, (j + 1) * B)
                out[p, c * B : (c + 1) * B, half] = env[table[p, 0, c * terms + j]][:, half]

    each(out.shape[0], fill)


def closed(products):
    return products[:B, :B] + pltpu.roll(products[B:, :], B, 1)[:, :B]


def image_kernel(slot, received, lcomb, image, wave, hpsi, rsel, stats, part):
    blocks = lcomb.shape[0]
    lanes = stats.shape[2]
    lane = lax.broadcasted_iota(jnp.int32, (1, lanes), 1)
    part[...] = jnp.zeros_like(part)

    def total(values):
        return jnp.sum(jnp.sum(values, axis=0, keepdims=True), axis=1, keepdims=True)

    def block(k):
        right = received[slot[k]]
        rsel[k] = right
        base = wave[k]
        h = closed(dot(image[k], right))
        hpsi[k] = h
        norm = total(base * base)
        cross = total(base * h)
        resid = h - cross / jnp.maximum(norm, TINY) * base
        zed = dot(resid.astype(BF16), right).astype(BF16)
        applied = closed(dot(lcomb[k], zed))
        sums = (
            norm,
            cross,
            total(resid * resid),
            total(resid * base),
            total(resid * applied),
            total(base * applied),
            total(resid * h),
        )
        here = lane == k
        for i, value in enumerate(sums):
            part[i : i + 1, :] = jnp.where(here, value, part[i : i + 1, :])

    each(blocks, block)
    whole = part[...]

    def spread(p):
        stats[p] = whole

    each(stats.shape[0], spread)


def second_kernel(count, stats, hpsi, wave, rsel, lcomb, second, direction, projected, stage, dir_stage):
    blocks = lcomb.shape[0]
    norm, cross, square, mixed, applied, crossed, image = (stats[:, i, :] for i in range(7))

    def total(values):
        return jnp.sum(jnp.sum(values, axis=0, keepdims=True), axis=1, keepdims=True)

    theta = total(cross) / total(norm)
    shift = theta - cross / jnp.maximum(norm, TINY)
    rr = total(square - 2.0 * shift * mixed + shift * shift * norm)
    along = total(applied - shift * (image + crossed) + shift * shift * cross)
    spread = rr / count
    projected[0] = theta[0, 0]
    projected[1] = jnp.sqrt(spread)[0, 0]
    projected[2] = (along / rr)[0, 0]
    scale = 1.0 / jnp.sqrt(spread + 1e-06)

    def block(k):
        place = pl.ds(pl.multiple_of(k * B, B), B)
        step = ((hpsi[k] - theta * wave[k]) * scale).astype(BF16)
        dir_stage[place, 0:B] = step.astype(F32)
        zed = dot(step, rsel[k]).astype(BF16)
        stage[place, 0:B] = closed(dot(lcomb[k], zed))

    each(blocks, block)
    low = lax.broadcasted_iota(jnp.int32, (8, LANES), 1) < B

    def rows(g):
        place = pl.ds(pl.multiple_of(8 * g, 8), 8)
        for t in range(B * B // LANES):
            base = 8 * g * B + 2 * t
            lanes = slice(t * LANES, (t + 1) * LANES)
            for source, target in ((stage, second), (dir_stage, direction)):
                even = source[pl.ds(base, 8, stride=B), :]
                odd = source[pl.ds(base + 1, 8, stride=B), :]
                target[place, lanes] = jnp.where(low, even, pltpu.roll(odd, B, 1)).astype(target.dtype)

    each(blocks // 8, rows)


VMEM = pl.BlockSpec(memory_space=pltpu.VMEM)
SMEM = pl.BlockSpec(memory_space=pltpu.SMEM)


def params(mib=40):
    return pltpu.CompilerParams(vmem_limit_bytes=mib << 20)


def per_device(psi, left_env, right_env, couple, left_sector, right_owner, right_local, channel):
    peers = lax.axis_size("sec")
    blocks = psi.shape[0]
    _, terms, chans = couple.shape
    lsecs = left_env.shape[0]
    rsecs = right_env.shape[0]
    slots = peers * CAP
    lanes = rounded_up(blocks, LANES)
    of = jax.ShapeDtypeStruct

    def exchange(values):
        return lax.all_to_all(values, "sec", split_axis=0, concat_axis=0, tiled=True)

    table, slot = pl.pallas_call(
        functools.partial(request_kernel, chans),
        out_shape=(of((peers, 1, CAP * terms), jnp.int32), of((blocks,), jnp.int32)),
        in_specs=[SMEM] * 3,
        out_specs=(SMEM, SMEM),
        scratch_shapes=[pltpu.SMEM((peers,), jnp.int32)],
        name="request",
    )(right_owner.T, right_local, channel.T)
    wanted = exchange(table)

    right = pl.pallas_call(
        right_kernel,
        grid=(rsecs,),
        out_shape=of((rsecs * chans, B, LANES), BF16),
        in_specs=[pl.BlockSpec((1, chans, B * B), lambda s: (s, 0, 0))],
        out_specs=pl.BlockSpec((chans, B, LANES), lambda s: (s, 0, 0)),
        scratch_shapes=[pltpu.VMEM((chans * B, LANES), F32)],
        compiler_params=params(),
        cost_estimate=pl.CostEstimate(flops=10_000_000, bytes_accessed=3_000_000, transcendentals=0),
        name="right",
    )(right_env)

    wide = rounded_up(lsecs * rounded_up(chans, 32), LANES)
    lcomb, image, wave = pl.pallas_call(
        left_kernel,
        out_shape=(
            of((blocks, terms * B, B), BF16),
            of((blocks, terms * B, B), BF16),
            of((blocks, B, B), F32),
        ),
        in_specs=[SMEM, VMEM, VMEM, VMEM],
        out_specs=(VMEM, VMEM, VMEM),
        scratch_shapes=[
            pltpu.VMEM((blocks * terms, wide), F32),
            pltpu.VMEM((wide, B * B), BF16),
            pltpu.VMEM((blocks * terms * B, LANES), F32),
            pltpu.VMEM((blocks * B, LANES), F32),
        ],
        compiler_params=params(),
        cost_estimate=pl.CostEstimate(flops=100_000_000, bytes_accessed=3_000_000, transcendentals=0),
        name="left",
    )(left_sector, couple, left_env, psi)

    sent = pl.pallas_call(
        gather_kernel,
        out_shape=of((peers, CAP * B, LANES), BF16),
        in_specs=[SMEM, VMEM],
        out_specs=VMEM,
        compiler_params=params(),
        name="gather",
    )(wanted, right)
    received = exchange(sent).reshape(slots, B, LANES)

    hpsi, rsel, stats = pl.pallas_call(
        image_kernel,
        out_shape=(
            of((blocks, B, B), F32),
            of((blocks, B, LANES), BF16),
            of((peers, STATS, lanes), F32),
        ),
        in_specs=[SMEM] + [VMEM] * 4,
        out_specs=(VMEM, VMEM, VMEM),
        scratch_shapes=[pltpu.VMEM((STATS, lanes), F32)],
        compiler_params=params(),
        name="image",
    )(slot, received, lcomb, image, wave)
    stats = exchange(stats)

    second, direction, projected = pl.pallas_call(
        functools.partial(second_kernel, float(blocks * peers * B * B)),
        out_shape=(of((blocks, B * B), F32), of((blocks, B * B), BF16), of((3,), F32)),
        in_specs=[VMEM] * 5,
        out_specs=(VMEM, VMEM, SMEM),
        scratch_shapes=[
            pltpu.VMEM((blocks * B, LANES), F32),
            pltpu.VMEM((blocks * B, LANES), F32),
        ],
        compiler_params=params(),
        name="second",
    )(stats, hpsi, wave, rsel, lcomb)
    return second, direction, projected


def solution(mesh):
    placed = (
        P(("parts", "sec"), None),
        P(("parts", "sec"), None, None),
        P(("parts", "sec"), None, None),
        P(("parts", "sec"), None, None),
        P(("parts", "sec")),
        P(("parts", "sec"), None),
        P(("parts", "sec")),
        P(("parts", "sec"), None),
    )
    return jax.shard_map(
        per_device,
        mesh=mesh,
        in_specs=placed,
        out_specs=(P(("parts", "sec"), None), P(("parts", "sec"), None), P("parts")),
        check_vma=False,
    )
```

```python
import functools

import jax
import jax.numpy as jnp
from jax import lax
from jax.experimental import pallas as pl
from jax.experimental.pallas import tpu as pltpu
from jax.sharding import PartitionSpec as P

B = 64
CAP = 2
LANES = 128
TILES = B * B // LANES
STATS = 7
SPACE = 16
TINY = 1e-30
F32 = jnp.float32
BF16 = jnp.bfloat16


def rounded_up(value, step):
    return -(-value // step) * step


def each(count, body):
    if count <= 32:
        for i in range(count):
            body(i)
    else:
        pl.loop(0, count)(body)


def dot(a, b):
    return jnp.dot(a, b, preferred_element_type=F32)


def low_half(rows=8):
    return lax.broadcasted_iota(jnp.int32, (rows, LANES), 1) < B


def swap(tile):
    return pltpu.roll(tile, B, 1)


def request_kernel(rsecs, owner, local, channel, table):
    terms, blocks = channel.shape
    peers = table.shape[0]
    peer = lax.broadcasted_iota(jnp.int32, (peers, LANES), 0)
    lane = lax.broadcasted_iota(jnp.int32, (peers, LANES), 1)
    wanted = channel[...] * rsecs + local[...]
    seen = jnp.zeros((peers, LANES), jnp.int32)
    filled = jnp.zeros((peers, LANES), jnp.int32)
    for k in range(blocks):
        hit = peer == owner[:, k : k + 1]
        for j in range(terms):
            filled = jnp.where(hit & (lane == seen * terms + j), wanted[j : j + 1, k : k + 1], filled)
        seen = seen + hit.astype(jnp.int32)
    table[...] = filled[:, : table.shape[1]]


def right_kernel(env, out, stage):
    chans, rsecs, _ = env.shape
    for w in range(chans):
        rows = env[w].astype(F32)
        for t in range(TILES):
            stage[pl.ds(w * rsecs * TILES + t, rsecs, stride=TILES), :] = rows[:, t * LANES : (t + 1) * LANES]
    out[...] = stage[...].reshape(out.shape).astype(BF16)


def gather_kernel(table, env, out):
    def fill(p):
        wanted = table[pl.ds(p, 1), :]
        for i in range(table.shape[1]):
            out[p, i * TILES : (i + 1) * TILES, :] = env[wanted[0, i]]

    each(out.shape[0], fill)


def left_kernel(sector, owner, couple, env, psi, lcomb, image, wave, slot, weights, envs, stage, twice):
    blocks, terms, chans = couple.shape
    lsecs = env.shape[0]
    wide = envs.shape[0]
    pitch = wide // lsecs
    rows = blocks * terms

    own = owner[...]
    lane = lax.broadcasted_iota(jnp.int32, own.shape, 1)
    rank = jnp.zeros_like(own)
    for k in range(blocks):
        rank = rank + ((own == own[:, k : k + 1]) & (lane > k)).astype(jnp.int32)
    slot[...] = own * CAP + rank

    weights[...] = jnp.zeros_like(weights)
    envs[...] = jnp.zeros_like(envs)
    for s in range(lsecs):
        envs[s * pitch : s * pitch + chans, :] = env[s]

    def weigh(k):
        for j in range(terms):
            weights[pl.ds(j * blocks + k, 1), 0:chans] = couple[k, j : j + 1]

    each(blocks, weigh)

    def turn(k):
        for j in range(terms):
            place = pl.ds(j * blocks + k, 1)
            weights[place, :] = pltpu.roll(weights[place, :], sector[k] * pitch, 1)

    each(blocks, turn)
    exact = weights[...]
    high = exact.astype(BF16)
    rest = exact - high.astype(F32)
    middle = rest.astype(BF16)
    low = (rest - middle.astype(F32)).astype(BF16)
    parts = jnp.concatenate([high, middle, low], axis=0)
    is_low = low_half()
    width = 512
    for n in range(B * B // width):
        sums = dot(parts, envs[:, n * width : (n + 1) * width])
        total = sums[:rows] + (sums[rows : 2 * rows] + sums[2 * rows :])
        for g in range(blocks // 8):
            for t in range(width // LANES):
                lanes = slice(t * LANES, (t + 1) * LANES)
                first = total[8 * g : 8 * g + 8, lanes]
                other = total[blocks + 8 * g : blocks + 8 * g + 8, lanes]
                base = 8 * g * B + 2 * (n * (width // LANES) + t)
                stage[pl.ds(base, 8, stride=B), :] = jnp.where(is_low, first, swap(other))
                stage[pl.ds(base + 1, 8, stride=B), :] = jnp.where(is_low, swap(first), other)

    def waves(g):
        held = psi[pl.ds(pl.multiple_of(8 * g, 8), 8), :].astype(F32)
        for t in range(TILES):
            tile = held[:, t * LANES : (t + 1) * LANES]
            base = 8 * g * B + 2 * t
            twice[pl.ds(base, 8, stride=B), :] = jnp.where(is_low, tile, swap(tile))
            twice[pl.ds(base + 1, 8, stride=B), :] = jnp.where(is_low, swap(tile), tile)

    each(blocks // 8, waves)
    left_lanes = low_half(B)

    def block(k):
        place = pl.ds(pl.multiple_of(k * B, B), B)
        left = stage[place, :].astype(BF16)
        base = twice[place, :]
        lcomb[k] = left
        wave[k] = base[:, :B]
        both = jnp.concatenate([jnp.where(left_lanes, base, 0.0), jnp.where(left_lanes, 0.0, base)], axis=0)
        image[k] = dot(left, both.astype(BF16)).astype(BF16)

    each(blocks, block)


def fold(values):
    return jnp.sum(values.reshape(B // 8, 8, B), axis=0)


def image_kernel(slot, received, lcomb, image, wave, hpsi, rsel, stats, stage, resid, zed, part):
    blocks = lcomb.shape[0]
    groups = blocks // 8
    places = slot[...]

    for k in range(blocks):
        raw = received[places[0, k]].astype(F32)
        stage[pl.ds(k * 2 * B, B, stride=2), :] = raw
        stage[pl.ds(k * 2 * B + 1, B, stride=2), :] = swap(raw)

    def unfold(k):
        rsel[k] = stage[pl.ds(pl.multiple_of(k * 2 * B, 2 * B), 2 * B), 0:B].astype(BF16)

    each(blocks, unfold)

    def keep(i, k, values):
        part[i, pl.ds(pl.multiple_of(k * 8, 8), 8), :] = fold(values)

    def of_group(i, g):
        sums = part[i, pl.ds(g * 8 * 8, 8, stride=8), :]
        for s in range(1, 8):
            sums = sums + part[i, pl.ds(g * 8 * 8 + s, 8, stride=8), :]
        return jnp.sum(sums, axis=1, keepdims=True)

    def apply(k):
        h = dot(image[k], rsel[k])
        base = wave[k]
        hpsi[k] = h
        keep(0, k, base * base)
        keep(1, k, base * h)

    each(blocks, apply)

    def group(g):
        norm, cross = of_group(0, g), of_group(1, g)
        theta = cross / jnp.maximum(norm, TINY)

        for i in range(8):
            k = g * 8 + i
            h, base = hpsi[k], wave[k]
            rest = h - theta[i : i + 1, :] * base
            resid[k] = rest
            step = rest.astype(BF16)
            zed[k, 0:B] = dot(step, rsel[k, 0:B]).astype(BF16)
            zed[k, B : 2 * B] = dot(step, rsel[k, B : 2 * B]).astype(BF16)
            keep(2, k, rest * rest)
            keep(3, k, rest * base)
            keep(4, k, rest * h)

        for i in range(8):
            k = g * 8 + i
            applied = dot(lcomb[k], zed[k])
            keep(5, k, resid[k] * applied)
            keep(6, k, wave[k] * applied)

        lane = lax.broadcasted_iota(jnp.int32, (8, LANES), 1)
        packed = jnp.zeros((8, LANES), F32)
        for i, value in enumerate([norm, cross] + [of_group(i, g) for i in range(2, STATS)]):
            packed = jnp.where(lane == i, value, packed)
        spread = pltpu.roll(packed, 0, 1, stride=SPACE, stride_axis=0)
        row = jnp.sum(spread, axis=0, keepdims=True)
        if groups == 1:
            stats[...] = jnp.broadcast_to(row, stats.shape)
        else:
            pl.loop(0, stats.shape[0] // groups)(lambda p: stats.__setitem__((pl.ds(p * groups + g, 1), slice(None)), row))

    each(groups, group)


def second_kernel(count, stats, hpsi, wave, rsel, lcomb, second, direction, projected, stage, steps, zed, narrow):
    blocks = lcomb.shape[0]
    held = stats[...]
    here = lax.broadcasted_iota(jnp.int32, held.shape, 1) % SPACE == 0
    norm, cross, square, mixed, image, applied, crossed = (
        jnp.where(here, pltpu.roll(held, (LANES - i) % LANES, 1) if i else held, 0.0) for i in range(STATS)
    )

    def total(values):
        return jnp.sum(jnp.sum(values, axis=0, keepdims=True), axis=1, keepdims=True)

    theta = total(cross) / total(norm)
    shift = theta - cross / jnp.maximum(norm, TINY)
    rr = total(square - 2.0 * shift * mixed + shift * shift * norm)
    along = total(applied - shift * (image + crossed) + shift * shift * cross)
    spread = rr / count
    scale = 1.0 / jnp.sqrt(spread + 1e-06)

    def move(k):
        place = pl.ds(pl.multiple_of(k * B, B), B)
        step = ((hpsi[k] - theta * wave[k]) * scale).astype(BF16)
        narrow[k] = step
        steps[place, 0:B] = step.astype(F32)

    each(blocks, move)

    def apply(k):
        zed[k, 0:B] = dot(narrow[k], rsel[k, 0:B]).astype(BF16)
        zed[k, B : 2 * B] = dot(narrow[k], rsel[k, B : 2 * B]).astype(BF16)

    each(blocks, apply)

    def close(k):
        stage[pl.ds(pl.multiple_of(k * B, B), B), 0:B] = dot(lcomb[k], zed[k])

    each(blocks, close)
    is_low = low_half()

    def rows(g):
        place = pl.ds(pl.multiple_of(8 * g, 8), 8)
        for source, target in ((steps, direction), (stage, second)):
            for t in range(TILES):
                base = 8 * g * B + 2 * t
                even = source[pl.ds(base, 8, stride=B), :]
                odd = source[pl.ds(base + 1, 8, stride=B), :]
                target[place, t * LANES : (t + 1) * LANES] = jnp.where(is_low, even, swap(odd)).astype(target.dtype)

    each(blocks // 8, rows)
    projected[0] = theta[0, 0]
    projected[1] = jnp.sqrt(spread)[0, 0]
    projected[2] = (along / rr)[0, 0]


VMEM = pl.BlockSpec(memory_space=pltpu.VMEM)
SMEM = pl.BlockSpec(memory_space=pltpu.SMEM)


def params(mib):
    return pltpu.CompilerParams(vmem_limit_bytes=mib << 20)


def cost(flops, moved):
    return pl.CostEstimate(flops=flops, bytes_accessed=moved, transcendentals=0)


def per_device(psi, left_env, right_env, couple, left_sector, right_owner, right_local, channel):
    peers = lax.axis_size("sec")
    blocks = psi.shape[0]
    _, terms, chans = couple.shape
    lsecs = left_env.shape[0]
    rsecs = right_env.shape[0]
    slots = peers * CAP
    groups = blocks // 8
    of = jax.ShapeDtypeStruct

    def exchange(values):
        return lax.all_to_all(values, "sec", split_axis=0, concat_axis=0, tiled=True)

    owner = right_owner.T
    table = pl.pallas_call(
        functools.partial(request_kernel, rsecs),
        out_shape=of((peers, CAP * terms), jnp.int32),
        in_specs=[VMEM] * 3,
        out_specs=VMEM,
        compiler_params=params(4),
        name="request",
    )(owner, right_local.reshape(1, blocks), channel.T)
    wanted = exchange(table.reshape(peers, 1, CAP * terms)).reshape(peers, CAP * terms)

    right = pl.pallas_call(
        right_kernel,
        out_shape=of((rsecs * chans, TILES, LANES), BF16),
        in_specs=[VMEM],
        out_specs=VMEM,
        scratch_shapes=[pltpu.VMEM((rsecs * chans * TILES, LANES), F32)],
        compiler_params=params(8),
        cost_estimate=cost(10_000_000, 3_000_000),
        name="right",
    )(right_env.transpose(1, 0, 2))

    wide = rounded_up(lsecs * rounded_up(chans, 32), LANES)
    lcomb, image, wave, slot = pl.pallas_call(
        left_kernel,
        out_shape=(
            of((blocks, B, terms * B), BF16),
            of((blocks, B, terms * B), BF16),
            of((blocks, B, B), F32),
            of((1, blocks), jnp.int32),
        ),
        in_specs=[SMEM, VMEM, VMEM, VMEM, VMEM],
        out_specs=(VMEM,) * 4,
        scratch_shapes=[
            pltpu.VMEM((blocks * terms, wide), F32),
            pltpu.VMEM((wide, B * B), BF16),
            pltpu.VMEM((blocks * B, LANES), F32),
            pltpu.VMEM((blocks * B, LANES), F32),
        ],
        compiler_params=params(24),
        cost_estimate=cost(100_000_000, 3_000_000),
        name="left",
    )(left_sector, owner, couple, left_env, psi)

    sent = pl.pallas_call(
        gather_kernel,
        out_shape=of((peers, CAP * terms * TILES, LANES), BF16),
        in_specs=[VMEM, VMEM],
        out_specs=VMEM,
        compiler_params=params(8),
        name="gather",
    )(wanted, right)
    received = exchange(sent).reshape(slots, terms * TILES, LANES)

    hpsi, rsel, stats = pl.pallas_call(
        image_kernel,
        out_shape=(
            of((blocks, B, B), F32),
            of((blocks, terms * B, B), BF16),
            of((peers * groups, LANES), F32),
        ),
        in_specs=[VMEM] * 5,
        out_specs=(VMEM, VMEM, VMEM),
        scratch_shapes=[
            pltpu.VMEM((blocks * terms * B, LANES), F32),
            pltpu.VMEM((blocks, B, B), F32),
            pltpu.VMEM((blocks, terms * B, B), BF16),
            pltpu.VMEM((STATS, blocks * 8, B), F32),
        ],
        compiler_params=params(24),
        name="image",
    )(slot, received, lcomb, image, wave)
    stats = exchange(stats.reshape(peers, groups, LANES)).reshape(peers * groups, LANES)

    second, direction, projected = pl.pallas_call(
        functools.partial(second_kernel, float(blocks * peers * B * B)),
        out_shape=(of((blocks, B * B), F32), of((blocks, B * B), BF16), of((3,), F32)),
        in_specs=[VMEM] * 5,
        out_specs=(VMEM, VMEM, SMEM),
        scratch_shapes=[
            pltpu.VMEM((blocks * B, LANES), F32),
            pltpu.VMEM((blocks * B, LANES), F32),
            pltpu.VMEM((blocks, terms * B, B), BF16),
            pltpu.VMEM((blocks, B, B), BF16),
        ],
        compiler_params=params(24),
        name="second",
    )(stats, hpsi, wave, rsel, lcomb)
    return second, direction, projected


def solution(mesh):
    placed = (
        P(("parts", "sec"), None),
        P(("parts", "sec"), None, None),
        P(("parts", "sec"), None, None),
        P(("parts", "sec"), None, None),
        P(("parts", "sec")),
        P(("parts", "sec"), None),
        P(("parts", "sec")),
        P(("parts", "sec"), None),
    )
    return jax.shard_map(
        per_device,
        mesh=mesh,
        in_specs=placed,
        out_specs=(P(("parts", "sec"), None), P(("parts", "sec"), None), P("parts")),
        check_vma=False,
    )
```

```python
import functools

import jax
import jax.numpy as jnp
from jax import lax
from jax.experimental import pallas as pl
from jax.experimental.pallas import tpu as pltpu
from jax.sharding import PartitionSpec as P

B = 64
CAP = 2
LANES = 128
TILES = B * B // LANES
STATS = 7
SPACE = 16
TINY = 1e-30
TABLE_ORDER = (9, 11, 12, 15, 0, 14, 6, 1, 8, 3, 4, 10, 7, 5, 13, 2)
MATRIX_ORDER = (9, 11, 5, 15, 12, 8, 6, 1, 10, 3, 4, 14, 7, 0, 13, 2)
SUM_ORDER = (9, 6, 0, 3, 11, 2, 4, 14, 1, 10, 12, 15, 8, 7, 13, 5)
F32 = jnp.float32
BF16 = jnp.bfloat16


def rounded_up(value, step):
    return -(-value // step) * step


def each(count, body):
    if count <= 32:
        for i in range(count):
            body(i)
    else:
        pl.loop(0, count)(body)


def run_of(order, peers):
    return 0 if peers % len(order) else peers // len(order)


def listed(order, peers):
    run = run_of(order, peers)
    return [q * run + i for q in order for i in range(run)] if run else list(range(peers))


def replaced(values, pairs, run):
    if not run:
        return values
    whole = values // run if run > 1 else values
    moved = values
    for old, new in pairs:
        moved = jnp.where(whole == old, values + (new - old) * run, moved)
    return moved


def dot(a, b):
    return jnp.dot(a, b, preferred_element_type=F32)


def low_half(rows=8):
    return lax.broadcasted_iota(jnp.int32, (rows, LANES), 1) < B


def swap(tile):
    return pltpu.roll(tile, B, 1)


def request_kernel(rsecs, owner, local, channel, table):
    terms, blocks = channel.shape
    peers = table.shape[0]
    peer = lax.broadcasted_iota(jnp.int32, (peers, LANES), 0)
    peer = replaced(peer, enumerate(TABLE_ORDER), run_of(TABLE_ORDER, peers))
    lane = lax.broadcasted_iota(jnp.int32, (peers, LANES), 1)
    wanted = channel[...] * rsecs + local[...]
    seen = jnp.zeros((peers, LANES), jnp.int32)
    filled = jnp.zeros((peers, LANES), jnp.int32)
    for k in range(blocks):
        hit = peer == owner[:, k : k + 1]
        for j in range(terms):
            filled = jnp.where(hit & (lane == seen * terms + j), wanted[j : j + 1, k : k + 1], filled)
        seen = seen + hit.astype(jnp.int32)
    table[...] = filled[:, : table.shape[1]]


def right_kernel(env, out, stage):
    chans, rsecs, _ = env.shape
    for w in range(chans):
        rows = env[w].astype(F32)
        for t in range(TILES):
            stage[pl.ds(w * rsecs * TILES + t, rsecs, stride=TILES), :] = rows[:, t * LANES : (t + 1) * LANES]
    out[...] = stage[...].reshape(out.shape).astype(BF16)


def gather_kernel(table, env, out):
    peers = out.shape[0]
    run = run_of(MATRIX_ORDER, peers)
    starts = [(q * run, TABLE_ORDER.index(peer) * run) for q, peer in enumerate(MATRIX_ORDER)] if run else [(0, 0)]
    for target, source in starts:

        def fill(p):
            wanted = table[pl.ds(source + p, 1), :]
            for i in range(table.shape[1]):
                out[target + p, i * TILES : (i + 1) * TILES, :] = env[wanted[0, i]]

        each(run or peers, fill)


def left_kernel(peers, sector, owner, couple, env, psi, lcomb, image, wave, slot, weights, envs, stage, twice):
    blocks, terms, chans = couple.shape
    lsecs = env.shape[0]
    wide = envs.shape[0]
    pitch = wide // lsecs
    rows = blocks * terms

    own = owner[...]
    lane = lax.broadcasted_iota(jnp.int32, own.shape, 1)
    rank = jnp.zeros_like(own)
    for k in range(blocks):
        rank = rank + ((own == own[:, k : k + 1]) & (lane > k)).astype(jnp.int32)
    place = [(peer, q) for q, peer in enumerate(MATRIX_ORDER)]
    slot[...] = replaced(own, place, run_of(MATRIX_ORDER, peers)) * CAP + rank

    weights[...] = jnp.zeros_like(weights)
    envs[...] = jnp.zeros_like(envs)
    for s in range(lsecs):
        envs[s * pitch : s * pitch + chans, :] = env[s]

    def weigh(k):
        for j in range(terms):
            weights[pl.ds(j * blocks + k, 1), 0:chans] = couple[k, j : j + 1]

    each(blocks, weigh)

    def turn(k):
        for j in range(terms):
            place = pl.ds(j * blocks + k, 1)
            weights[place, :] = pltpu.roll(weights[place, :], sector[k] * pitch, 1)

    each(blocks, turn)
    exact = weights[...]
    high = exact.astype(BF16)
    rest = exact - high.astype(F32)
    middle = rest.astype(BF16)
    low = (rest - middle.astype(F32)).astype(BF16)
    parts = jnp.concatenate([high, middle, low], axis=0)
    is_low = low_half()
    width = 512
    for n in range(B * B // width):
        sums = dot(parts, envs[:, n * width : (n + 1) * width])
        total = sums[:rows] + (sums[rows : 2 * rows] + sums[2 * rows :])
        for g in range(blocks // 8):
            for t in range(width // LANES):
                lanes = slice(t * LANES, (t + 1) * LANES)
                first = total[8 * g : 8 * g + 8, lanes]
                other = total[blocks + 8 * g : blocks + 8 * g + 8, lanes]
                base = 8 * g * B + 2 * (n * (width // LANES) + t)
                stage[pl.ds(base, 8, stride=B), :] = jnp.where(is_low, first, swap(other))
                stage[pl.ds(base + 1, 8, stride=B), :] = jnp.where(is_low, swap(first), other)

    def waves(g):
        held = psi[pl.ds(pl.multiple_of(8 * g, 8), 8), :].astype(F32)
        for t in range(TILES):
            tile = held[:, t * LANES : (t + 1) * LANES]
            base = 8 * g * B + 2 * t
            twice[pl.ds(base, 8, stride=B), :] = jnp.where(is_low, tile, swap(tile))
            twice[pl.ds(base + 1, 8, stride=B), :] = jnp.where(is_low, swap(tile), tile)

    each(blocks // 8, waves)
    left_lanes = low_half(B)

    def block(k):
        place = pl.ds(pl.multiple_of(k * B, B), B)
        left = stage[place, :].astype(BF16)
        base = twice[place, :]
        lcomb[k] = left
        wave[k] = base[:, :B]
        both = jnp.concatenate([jnp.where(left_lanes, base, 0.0), jnp.where(left_lanes, 0.0, base)], axis=0)
        image[k] = dot(left, both.astype(BF16)).astype(BF16)

    each(blocks, block)


def fold(values):
    return jnp.sum(values.reshape(B // 8, 8, B), axis=0)


def image_kernel(slot, received, lcomb, image, wave, hpsi, rsel, stats, stage, resid, zed, part):
    blocks = lcomb.shape[0]
    groups = blocks // 8
    places = slot[...]

    for k in range(blocks):
        raw = received[places[0, k]].astype(F32)
        stage[pl.ds(k * 2 * B, B, stride=2), :] = raw
        stage[pl.ds(k * 2 * B + 1, B, stride=2), :] = swap(raw)

    def unfold(k):
        rsel[k] = stage[pl.ds(pl.multiple_of(k * 2 * B, 2 * B), 2 * B), 0:B].astype(BF16)

    each(blocks, unfold)

    def keep(i, k, values):
        part[i, pl.ds(pl.multiple_of(k * 8, 8), 8), :] = fold(values)

    def of_group(i, g):
        sums = part[i, pl.ds(g * 8 * 8, 8, stride=8), :]
        for s in range(1, 8):
            sums = sums + part[i, pl.ds(g * 8 * 8 + s, 8, stride=8), :]
        return jnp.sum(sums, axis=1, keepdims=True)

    def apply(k):
        h = dot(image[k], rsel[k])
        base = wave[k]
        hpsi[k] = h
        keep(0, k, base * base)
        keep(1, k, base * h)

    each(blocks, apply)

    def group(g):
        norm, cross = of_group(0, g), of_group(1, g)
        theta = cross / jnp.maximum(norm, TINY)

        for i in range(8):
            k = g * 8 + i
            h, base = hpsi[k], wave[k]
            rest = h - theta[i : i + 1, :] * base
            resid[k] = rest
            step = rest.astype(BF16)
            zed[k, 0:B] = dot(step, rsel[k, 0:B]).astype(BF16)
            zed[k, B : 2 * B] = dot(step, rsel[k, B : 2 * B]).astype(BF16)
            keep(2, k, rest * rest)
            keep(3, k, rest * base)
            keep(4, k, rest * h)

        for i in range(8):
            k = g * 8 + i
            applied = dot(lcomb[k], zed[k])
            keep(5, k, resid[k] * applied)
            keep(6, k, wave[k] * applied)

        lane = lax.broadcasted_iota(jnp.int32, (8, LANES), 1)
        packed = jnp.zeros((8, LANES), F32)
        for i, value in enumerate([norm, cross] + [of_group(i, g) for i in range(2, STATS)]):
            packed = jnp.where(lane == i, value, packed)
        spread = pltpu.roll(packed, 0, 1, stride=SPACE, stride_axis=0)
        row = jnp.sum(spread, axis=0, keepdims=True)
        if groups == 1:
            stats[...] = jnp.broadcast_to(row, stats.shape)
        else:
            pl.loop(0, stats.shape[0] // groups)(lambda p: stats.__setitem__((pl.ds(p * groups + g, 1), slice(None)), row))

    each(groups, group)


def second_kernel(count, stats, hpsi, wave, rsel, lcomb, second, direction, projected, stage, steps, zed, narrow):
    blocks = lcomb.shape[0]
    held = stats[...]
    here = lax.broadcasted_iota(jnp.int32, held.shape, 1) % SPACE == 0
    norm, cross, square, mixed, image, applied, crossed = (
        jnp.where(here, pltpu.roll(held, (LANES - i) % LANES, 1) if i else held, 0.0) for i in range(STATS)
    )

    def total(values):
        return jnp.sum(jnp.sum(values, axis=0, keepdims=True), axis=1, keepdims=True)

    theta = total(cross) / total(norm)
    shift = theta - cross / jnp.maximum(norm, TINY)
    rr = total(square - 2.0 * shift * mixed + shift * shift * norm)
    along = total(applied - shift * (image + crossed) + shift * shift * cross)
    spread = rr / count
    scale = 1.0 / jnp.sqrt(spread + 1e-06)

    def move(k):
        place = pl.ds(pl.multiple_of(k * B, B), B)
        step = ((hpsi[k] - theta * wave[k]) * scale).astype(BF16)
        narrow[k] = step
        steps[place, 0:B] = step.astype(F32)

    each(blocks, move)

    def apply(k):
        zed[k, 0:B] = dot(narrow[k], rsel[k, 0:B]).astype(BF16)
        zed[k, B : 2 * B] = dot(narrow[k], rsel[k, B : 2 * B]).astype(BF16)

    each(blocks, apply)

    def close(k):
        stage[pl.ds(pl.multiple_of(k * B, B), B), 0:B] = dot(lcomb[k], zed[k])

    each(blocks, close)
    is_low = low_half()

    def rows(g):
        place = pl.ds(pl.multiple_of(8 * g, 8), 8)
        for source, target in ((steps, direction), (stage, second)):
            for t in range(TILES):
                base = 8 * g * B + 2 * t
                even = source[pl.ds(base, 8, stride=B), :]
                odd = source[pl.ds(base + 1, 8, stride=B), :]
                target[place, t * LANES : (t + 1) * LANES] = jnp.where(is_low, even, swap(odd)).astype(target.dtype)

    each(blocks // 8, rows)
    projected[0] = theta[0, 0]
    projected[1] = jnp.sqrt(spread)[0, 0]
    projected[2] = (along / rr)[0, 0]


VMEM = pl.BlockSpec(memory_space=pltpu.VMEM)
SMEM = pl.BlockSpec(memory_space=pltpu.SMEM)


def params(mib):
    return pltpu.CompilerParams(vmem_limit_bytes=mib << 20)


def cost(flops, moved):
    return pl.CostEstimate(flops=flops, bytes_accessed=moved, transcendentals=0)


def per_device(psi, left_env, right_env, couple, left_sector, right_owner, right_local, channel):
    peers = lax.axis_size("sec")
    blocks = psi.shape[0]
    _, terms, chans = couple.shape
    lsecs = left_env.shape[0]
    rsecs = right_env.shape[0]
    slots = peers * CAP
    groups = blocks // 8
    of = jax.ShapeDtypeStruct

    def exchange(values, order):
        members = [listed(order, peers)]
        return lax.all_to_all(values, "sec", split_axis=0, concat_axis=0, axis_index_groups=members, tiled=True)

    owner = right_owner.T
    table = pl.pallas_call(
        functools.partial(request_kernel, rsecs),
        out_shape=of((peers, CAP * terms), jnp.int32),
        in_specs=[VMEM] * 3,
        out_specs=VMEM,
        compiler_params=params(4),
        name="request",
    )(owner, right_local.reshape(1, blocks), channel.T)
    wanted = exchange(table.reshape(peers, 1, CAP * terms), TABLE_ORDER).reshape(peers, CAP * terms)

    right = pl.pallas_call(
        right_kernel,
        out_shape=of((rsecs * chans, TILES, LANES), BF16),
        in_specs=[VMEM],
        out_specs=VMEM,
        scratch_shapes=[pltpu.VMEM((rsecs * chans * TILES, LANES), F32)],
        compiler_params=params(8),
        cost_estimate=cost(10_000_000, 3_000_000),
        name="right",
    )(right_env.transpose(1, 0, 2))

    wide = rounded_up(lsecs * rounded_up(chans, 32), LANES)
    lcomb, image, wave, slot = pl.pallas_call(
        functools.partial(left_kernel, peers),
        out_shape=(
            of((blocks, B, terms * B), BF16),
            of((blocks, B, terms * B), BF16),
            of((blocks, B, B), F32),
            of((1, blocks), jnp.int32),
        ),
        in_specs=[SMEM, VMEM, VMEM, VMEM, VMEM],
        out_specs=(VMEM,) * 4,
        scratch_shapes=[
            pltpu.VMEM((blocks * terms, wide), F32),
            pltpu.VMEM((wide, B * B), BF16),
            pltpu.VMEM((blocks * B, LANES), F32),
            pltpu.VMEM((blocks * B, LANES), F32),
        ],
        compiler_params=params(24),
        cost_estimate=cost(100_000_000, 3_000_000),
        name="left",
    )(left_sector, owner, couple, left_env, psi)

    sent = pl.pallas_call(
        gather_kernel,
        out_shape=of((peers, CAP * terms * TILES, LANES), BF16),
        in_specs=[VMEM, VMEM],
        out_specs=VMEM,
        compiler_params=params(8),
        name="gather",
    )(wanted, right)
    received = exchange(sent, MATRIX_ORDER).reshape(slots, terms * TILES, LANES)

    hpsi, rsel, stats = pl.pallas_call(
        image_kernel,
        out_shape=(
            of((blocks, B, B), F32),
            of((blocks, terms * B, B), BF16),
            of((peers * groups, LANES), F32),
        ),
        in_specs=[VMEM] * 5,
        out_specs=(VMEM, VMEM, VMEM),
        scratch_shapes=[
            pltpu.VMEM((blocks * terms * B, LANES), F32),
            pltpu.VMEM((blocks, B, B), F32),
            pltpu.VMEM((blocks, terms * B, B), BF16),
            pltpu.VMEM((STATS, blocks * 8, B), F32),
        ],
        compiler_params=params(24),
        name="image",
    )(slot, received, lcomb, image, wave)
    stats = exchange(stats.reshape(peers, groups, LANES), SUM_ORDER).reshape(peers * groups, LANES)

    second, direction, projected = pl.pallas_call(
        functools.partial(second_kernel, float(blocks * peers * B * B)),
        out_shape=(of((blocks, B * B), F32), of((blocks, B * B), BF16), of((3,), F32)),
        in_specs=[VMEM] * 5,
        out_specs=(VMEM, VMEM, SMEM),
        scratch_shapes=[
            pltpu.VMEM((blocks * B, LANES), F32),
            pltpu.VMEM((blocks * B, LANES), F32),
            pltpu.VMEM((blocks, terms * B, B), BF16),
            pltpu.VMEM((blocks, B, B), BF16),
        ],
        compiler_params=params(24),
        name="second",
    )(stats, hpsi, wave, rsel, lcomb)
    return second, direction, projected


def solution(mesh):
    placed = (
        P(("parts", "sec"), None),
        P(("parts", "sec"), None, None),
        P(("parts", "sec"), None, None),
        P(("parts", "sec"), None, None),
        P(("parts", "sec")),
        P(("parts", "sec"), None),
        P(("parts", "sec")),
        P(("parts", "sec"), None),
    )
    return jax.shard_map(
        per_device,
        mesh=mesh,
        in_specs=placed,
        out_specs=(P(("parts", "sec"), None), P(("parts", "sec"), None), P("parts")),
        check_vma=False,
    )
```

```python
import functools

import jax
import jax.numpy as jnp
from jax import lax
from jax.experimental import pallas as pl
from jax.experimental.pallas import tpu as pltpu
from jax.sharding import PartitionSpec as P

B = 64
CAP = 2
LANES = 128
TILES = B * B // LANES
STATS = 7
SPACE = 16
TINY = 1e-30
TABLE_ORDER = (9, 11, 12, 15, 0, 14, 6, 1, 8, 3, 4, 10, 7, 5, 13, 2)
MATRIX_ORDER = (9, 11, 5, 15, 12, 8, 6, 1, 10, 3, 4, 14, 7, 0, 13, 2)
SUM_ORDER = (9, 6, 0, 3, 11, 2, 4, 14, 1, 10, 12, 15, 8, 7, 13, 5)
F32 = jnp.float32
BF16 = jnp.bfloat16


def rounded_up(value, step):
    return -(-value // step) * step


def each(count, body):
    if count <= 32:
        for i in range(count):
            body(i)
    else:
        pl.loop(0, count)(body)


def run_of(order, peers):
    return 0 if peers % len(order) else peers // len(order)


def listed(order, peers):
    run = run_of(order, peers)
    return [q * run + i for q in order for i in range(run)] if run else list(range(peers))


def replaced(values, pairs, run):
    if not run:
        return values
    whole = values // run if run > 1 else values
    moved = values
    for old, new in pairs:
        moved = jnp.where(whole == old, values + (new - old) * run, moved)
    return moved


def dot(a, b):
    return jnp.dot(a, b, preferred_element_type=F32)


def low_half(rows=8):
    return lax.broadcasted_iota(jnp.int32, (rows, LANES), 1) < B


def swap(tile):
    return pltpu.roll(tile, B, 1)


def request_kernel(rsecs, owner, local, channel, table):
    terms, blocks = channel.shape
    peers = table.shape[0]
    peer = lax.broadcasted_iota(jnp.int32, (peers, LANES), 0)
    peer = replaced(peer, enumerate(TABLE_ORDER), run_of(TABLE_ORDER, peers))
    lane = lax.broadcasted_iota(jnp.int32, (peers, LANES), 1)
    wanted = channel[...] * rsecs + local[...]
    seen = jnp.zeros((peers, LANES), jnp.int32)
    filled = jnp.zeros((peers, LANES), jnp.int32)
    for k in range(blocks):
        hit = peer == owner[:, k : k + 1]
        for j in range(terms):
            filled = jnp.where(hit & (lane == seen * terms + j), wanted[j : j + 1, k : k + 1], filled)
        seen = seen + hit.astype(jnp.int32)
    table[...] = filled[:, : table.shape[1]]


def gather_kernel(table, env, out):
    peers = out.shape[0]
    run = run_of(MATRIX_ORDER, peers)
    starts = [(q * run, TABLE_ORDER.index(peer) * run) for q, peer in enumerate(MATRIX_ORDER)] if run else [(0, 0)]
    for target, source in starts:

        def fill(p):
            wanted = table[pl.ds(source + p, 1), :]
            for i in range(table.shape[1]):
                out[target + p, i * TILES : (i + 1) * TILES, :] = env[wanted[0, i]]

        each(run or peers, fill)


def prepare_kernel(
    peers, sector_far, owner_far, couple_far, psi_far, left_far, right_far, right, lcomb, image, wave, slot,
    sector, owner, couple, psi, left_env, right_env, arrived, flat, right_stage, stage, twice,
):
    blocks, terms, chans = couple.shape
    lsecs = left_env.shape[1]
    rsecs = right_env.shape[1]
    wide = flat.shape[0]
    rows = blocks * terms
    moves = [
        pltpu.make_async_copy(source, target, arrived.at[i])
        for i, (source, target) in enumerate(
            (
                (right_far, right_env),
                (left_far, left_env),
                (psi_far, psi),
                (couple_far, couple),
                (sector_far, sector),
                (owner_far, owner),
            )
        )
    ]
    for move in moves:
        move.start()
    flat[chans * lsecs :, :] = jnp.zeros((wide - chans * lsecs, B * B), F32)
    moves[0].wait()

    for w in range(chans):
        slab = right_env[w].astype(F32)
        for t in range(TILES):
            right_stage[pl.ds(w * rsecs * TILES + t, rsecs, stride=TILES), :] = slab[:, t * LANES : (t + 1) * LANES]
    right[...] = right_stage[...].reshape(right.shape).astype(BF16)

    for move in moves[1:]:
        move.wait()
    own = owner[...]
    lane = lax.broadcasted_iota(jnp.int32, own.shape, 1)
    rank = jnp.zeros_like(own)
    for k in range(blocks):
        rank = rank + ((own == own[:, k : k + 1]) & (lane > k)).astype(jnp.int32)
    place = [(peer, q) for q, peer in enumerate(MATRIX_ORDER)]
    slot[...] = replaced(own, place, run_of(MATRIX_ORDER, peers)) * CAP + rank

    is_low = low_half()

    waves = psi[...].astype(F32)
    for g in range(blocks // 8):
        for t in range(TILES):
            tile = waves[8 * g : 8 * g + 8, t * LANES : (t + 1) * LANES]
            base = 8 * g * B + 2 * t
            twice[pl.ds(base, 8, stride=B), :] = jnp.where(is_low, tile, swap(tile))
            twice[pl.ds(base + 1, 8, stride=B), :] = jnp.where(is_low, swap(tile), tile)

    exact = jnp.concatenate([couple[:, j, :] for j in range(terms)], axis=0)
    high = exact.astype(BF16)
    rest = exact - high.astype(F32)
    middle = rest.astype(BF16)
    low = (rest - middle.astype(F32)).astype(BF16)
    column = lax.broadcasted_iota(jnp.int32, (chans, wide), 1)
    begin = lax.broadcasted_iota(jnp.int32, (chans, wide), 0) * lsecs
    spreads = ((column >= begin) & (column < begin + lsecs)).astype(F32).astype(BF16)
    wider = dot(jnp.concatenate([high, middle, low], axis=0), spreads)
    row = lax.broadcasted_iota(jnp.int32, (blocks, wide), 0)
    of_lane = lax.rem(lax.broadcasted_iota(jnp.int32, (blocks, wide), 1), lsecs)
    own_sector = sector[...]
    chosen = jnp.zeros((blocks, wide), jnp.int32)
    for k in range(blocks):
        chosen = jnp.where(row == k, own_sector[:, k : k + 1], chosen)
    mask = (chosen == of_lane).astype(F32)
    parts = (wider * jnp.concatenate([mask] * (3 * terms), axis=0)).astype(BF16)

    for w in range(chans):
        flat[w * lsecs : (w + 1) * lsecs, :] = left_env[w].astype(F32)
    width = 512
    for n in range(B * B // width):
        sums = dot(parts, flat[:, n * width : (n + 1) * width].astype(BF16))
        total = sums[:rows] + (sums[rows : 2 * rows] + sums[2 * rows :])
        for g in range(blocks // 8):
            for t in range(width // LANES):
                lanes = slice(t * LANES, (t + 1) * LANES)
                first = total[8 * g : 8 * g + 8, lanes]
                other = total[blocks + 8 * g : blocks + 8 * g + 8, lanes]
                base = 8 * g * B + 2 * (n * (width // LANES) + t)
                stage[pl.ds(base, 8, stride=B), :] = jnp.where(is_low, first, swap(other))
                stage[pl.ds(base + 1, 8, stride=B), :] = jnp.where(is_low, swap(first), other)

    left_lanes = low_half(B)

    def block(k):
        place = pl.ds(pl.multiple_of(k * B, B), B)
        left = stage[place, :].astype(BF16)
        base = twice[place, :]
        lcomb[k] = left
        wave[k] = base[:, :B]
        both = jnp.concatenate([jnp.where(left_lanes, base, 0.0), jnp.where(left_lanes, 0.0, base)], axis=0)
        image[k] = dot(left, both.astype(BF16)).astype(BF16)

    each(blocks, block)


def fold(values):
    return jnp.sum(values.reshape(B // 8, 8, B), axis=0)


def image_kernel(slot, received, lcomb, image, wave, hpsi, rsel, stats, stage, resid, zed, part):
    blocks = lcomb.shape[0]
    groups = blocks // 8
    places = slot[...]

    for k in range(blocks):
        raw = received[places[0, k]].astype(F32)
        stage[pl.ds(k * 2 * B, B, stride=2), :] = raw
        stage[pl.ds(k * 2 * B + 1, B, stride=2), :] = swap(raw)

    def unfold(k):
        rsel[k] = stage[pl.ds(pl.multiple_of(k * 2 * B, 2 * B), 2 * B), 0:B].astype(BF16)

    each(blocks, unfold)

    def keep(i, k, values):
        part[i, pl.ds(pl.multiple_of(k * 8, 8), 8), :] = fold(values)

    def of_group(i, g):
        sums = part[i, pl.ds(g * 8 * 8, 8, stride=8), :]
        for s in range(1, 8):
            sums = sums + part[i, pl.ds(g * 8 * 8 + s, 8, stride=8), :]
        return jnp.sum(sums, axis=1, keepdims=True)

    def apply(k):
        h = dot(image[k], rsel[k])
        base = wave[k]
        hpsi[k] = h
        keep(0, k, base * base)
        keep(1, k, base * h)

    each(blocks, apply)

    def group(g):
        norm, cross = of_group(0, g), of_group(1, g)
        theta = cross / jnp.maximum(norm, TINY)

        for i in range(8):
            k = g * 8 + i
            h, base = hpsi[k], wave[k]
            rest = h - theta[i : i + 1, :] * base
            resid[k] = rest
            step = rest.astype(BF16)
            zed[k, 0:B] = dot(step, rsel[k, 0:B]).astype(BF16)
            zed[k, B : 2 * B] = dot(step, rsel[k, B : 2 * B]).astype(BF16)
            keep(2, k, rest * rest)
            keep(3, k, rest * base)
            keep(4, k, rest * h)

        for i in range(8):
            k = g * 8 + i
            applied = dot(lcomb[k], zed[k])
            keep(5, k, resid[k] * applied)
            keep(6, k, wave[k] * applied)

        lane = lax.broadcasted_iota(jnp.int32, (8, LANES), 1)
        packed = jnp.zeros((8, LANES), F32)
        for i, value in enumerate([norm, cross] + [of_group(i, g) for i in range(2, STATS)]):
            packed = jnp.where(lane == i, value, packed)
        spread = pltpu.roll(packed, 0, 1, stride=SPACE, stride_axis=0)
        row = jnp.sum(spread, axis=0, keepdims=True)
        if groups == 1:
            stats[...] = jnp.broadcast_to(row, stats.shape)
        else:
            pl.loop(0, stats.shape[0] // groups)(lambda p: stats.__setitem__((pl.ds(p * groups + g, 1), slice(None)), row))

    each(groups, group)


def second_kernel(count, stats, hpsi, wave, rsel, lcomb, second, direction, projected, stage, steps, zed, narrow):
    blocks = lcomb.shape[0]
    held = stats[...]
    here = lax.broadcasted_iota(jnp.int32, held.shape, 1) % SPACE == 0
    norm, cross, square, mixed, image, applied, crossed = (
        jnp.where(here, pltpu.roll(held, (LANES - i) % LANES, 1) if i else held, 0.0) for i in range(STATS)
    )

    def total(values):
        return jnp.sum(jnp.sum(values, axis=0, keepdims=True), axis=1, keepdims=True)

    theta = total(cross) / total(norm)
    shift = theta - cross / jnp.maximum(norm, TINY)
    rr = total(square - 2.0 * shift * mixed + shift * shift * norm)
    along = total(applied - shift * (image + crossed) + shift * shift * cross)
    spread = rr / count
    scale = 1.0 / jnp.sqrt(spread + 1e-06)

    def move(k):
        place = pl.ds(pl.multiple_of(k * B, B), B)
        step = ((hpsi[k] - theta * wave[k]) * scale).astype(BF16)
        narrow[k] = step
        steps[place, 0:B] = step.astype(F32)

    each(blocks, move)

    def apply(k):
        zed[k, 0:B] = dot(narrow[k], rsel[k, 0:B]).astype(BF16)
        zed[k, B : 2 * B] = dot(narrow[k], rsel[k, B : 2 * B]).astype(BF16)

    each(blocks, apply)

    def close(k):
        stage[pl.ds(pl.multiple_of(k * B, B), B), 0:B] = dot(lcomb[k], zed[k])

    each(blocks, close)
    is_low = low_half()

    def rows(g):
        place = pl.ds(pl.multiple_of(8 * g, 8), 8)
        for source, target in ((steps, direction), (stage, second)):
            for t in range(TILES):
                base = 8 * g * B + 2 * t
                even = source[pl.ds(base, 8, stride=B), :]
                odd = source[pl.ds(base + 1, 8, stride=B), :]
                target[place, t * LANES : (t + 1) * LANES] = jnp.where(is_low, even, swap(odd)).astype(target.dtype)

    each(blocks // 8, rows)
    projected[0] = theta[0, 0]
    projected[1] = jnp.sqrt(spread)[0, 0]
    projected[2] = (along / rr)[0, 0]


VMEM = pl.BlockSpec(memory_space=pltpu.VMEM)
SMEM = pl.BlockSpec(memory_space=pltpu.SMEM)


def params(mib):
    return pltpu.CompilerParams(vmem_limit_bytes=mib << 20)


def cost(flops, moved):
    return pl.CostEstimate(flops=flops, bytes_accessed=moved, transcendentals=0)


def per_device(psi, left_env, right_env, couple, left_sector, right_owner, right_local, channel):
    peers = lax.axis_size("sec")
    blocks = psi.shape[0]
    _, terms, chans = couple.shape
    lsecs = left_env.shape[0]
    rsecs = right_env.shape[0]
    slots = peers * CAP
    groups = blocks // 8
    of = jax.ShapeDtypeStruct

    def exchange(values, order):
        members = [listed(order, peers)]
        return lax.all_to_all(values, "sec", split_axis=0, concat_axis=0, axis_index_groups=members, tiled=True)

    owner = right_owner.T
    table = pl.pallas_call(
        functools.partial(request_kernel, rsecs),
        out_shape=of((peers, CAP * terms), jnp.int32),
        in_specs=[VMEM] * 3,
        out_specs=VMEM,
        compiler_params=params(4),
        cost_estimate=cost(0, 0),
        name="request",
    )(owner, right_local.reshape(1, blocks), channel.T)
    wanted = exchange(table.reshape(peers, 1, CAP * terms), TABLE_ORDER).reshape(peers, CAP * terms)

    wide = rounded_up(lsecs * chans, LANES)
    inputs = (
        left_sector.reshape(1, blocks),
        owner,
        couple,
        psi,
        left_env.transpose(1, 0, 2),
        right_env.transpose(1, 0, 2),
    )
    right, lcomb, image, wave, slot = pl.pallas_call(
        functools.partial(prepare_kernel, peers),
        out_shape=(
            of((chans * rsecs, TILES, LANES), BF16),
            of((blocks, B, terms * B), BF16),
            of((blocks, B, terms * B), BF16),
            of((blocks, B, B), F32),
            of((1, blocks), jnp.int32),
        ),
        in_specs=[pl.BlockSpec(memory_space=pl.ANY)] * len(inputs),
        out_specs=(VMEM,) * 5,
        scratch_shapes=[pltpu.VMEM(x.shape, x.dtype) for x in inputs]
        + [
            pltpu.SemaphoreType.DMA((len(inputs),)),
            pltpu.VMEM((wide, B * B), F32),
            pltpu.VMEM((chans * rsecs * TILES, LANES), F32),
            pltpu.VMEM((blocks * B, LANES), F32),
            pltpu.VMEM((blocks * B, LANES), F32),
        ],
        compiler_params=params(24),
        cost_estimate=cost(100_000_000, 3_000_000),
        name="prepare",
    )(*[pltpu.with_memory_space_constraint(x, pltpu.HBM) for x in inputs])

    sent = pl.pallas_call(
        gather_kernel,
        out_shape=of((peers, CAP * terms * TILES, LANES), BF16),
        in_specs=[VMEM, VMEM],
        out_specs=VMEM,
        compiler_params=params(8),
        name="gather",
    )(wanted, right)
    received = exchange(sent, MATRIX_ORDER).reshape(slots, terms * TILES, LANES)

    hpsi, rsel, stats = pl.pallas_call(
        image_kernel,
        out_shape=(
            of((blocks, B, B), F32),
            of((blocks, terms * B, B), BF16),
            of((peers * groups, LANES), F32),
        ),
        in_specs=[VMEM] * 5,
        out_specs=(VMEM, VMEM, VMEM),
        scratch_shapes=[
            pltpu.VMEM((blocks * terms * B, LANES), F32),
            pltpu.VMEM((blocks, B, B), F32),
            pltpu.VMEM((blocks, terms * B, B), BF16),
            pltpu.VMEM((STATS, blocks * 8, B), F32),
        ],
        compiler_params=params(24),
        name="image",
    )(slot, received, lcomb, image, wave)
    stats = exchange(stats.reshape(peers, groups, LANES), SUM_ORDER).reshape(peers * groups, LANES)

    second, direction, projected = pl.pallas_call(
        functools.partial(second_kernel, float(blocks * peers * B * B)),
        out_shape=(of((blocks, B * B), F32), of((blocks, B * B), BF16), of((3,), F32)),
        in_specs=[VMEM] * 5,
        out_specs=(VMEM, VMEM, SMEM),
        scratch_shapes=[
            pltpu.VMEM((blocks * B, LANES), F32),
            pltpu.VMEM((blocks * B, LANES), F32),
            pltpu.VMEM((blocks, terms * B, B), BF16),
            pltpu.VMEM((blocks, B, B), BF16),
        ],
        compiler_params=params(24),
        name="second",
    )(stats, hpsi, wave, rsel, lcomb)
    return second, direction, projected


def solution(mesh):
    placed = (
        P(("parts", "sec"), None),
        P(("parts", "sec"), None, None),
        P(("parts", "sec"), None, None),
        P(("parts", "sec"), None, None),
        P(("parts", "sec")),
        P(("parts", "sec"), None),
        P(("parts", "sec")),
        P(("parts", "sec"), None),
    )
    return jax.shard_map(
        per_device,
        mesh=mesh,
        in_specs=placed,
        out_specs=(P(("parts", "sec"), None), P(("parts", "sec"), None), P("parts")),
        check_vma=False,
    )
```

```python
import functools

import jax
import jax.numpy as jnp
from jax import lax
from jax.experimental import pallas as pl
from jax.experimental.pallas import tpu as pltpu
from jax.sharding import PartitionSpec as P

B = 64
CAP = 2
LANES = 128
TILES = B * B // LANES
STATS = 7
SPACE = 16
TINY = 1e-30
ORDER = (11, 2, 14, 6, 9, 7, 13, 10, 8, 5, 4, 12, 1, 15, 0, 3)
F32 = jnp.float32
BF16 = jnp.bfloat16


def rounded_up(value, step):
    return -(-value // step) * step


def each(count, body):
    if count <= 32:
        for i in range(count):
            body(i)
    else:
        pl.loop(0, count)(body)


def run_of(peers):
    return 0 if peers % len(ORDER) else peers // len(ORDER)


def listed(peers):
    run = run_of(peers)
    return [q * run + i for q in ORDER for i in range(run)] if run else list(range(peers))


def replaced(values, pairs, peers):
    run = run_of(peers)
    if not run:
        return values
    whole = values // run if run > 1 else values
    moved = values
    for old, new in pairs:
        moved = jnp.where(whole == old, values + (new - old) * run, moved)
    return moved


def dot(a, b):
    return jnp.dot(a, b, preferred_element_type=F32)


def low_half(rows=8):
    return lax.broadcasted_iota(jnp.int32, (rows, LANES), 1) < B


def swap(tile):
    return pltpu.roll(tile, B, 1)


def request_kernel(rsecs, owner, local, channel, table):
    terms, blocks = channel.shape
    peers = table.shape[0]
    peer = lax.broadcasted_iota(jnp.int32, (peers, LANES), 0)
    peer = replaced(peer, enumerate(ORDER), peers)
    lane = lax.broadcasted_iota(jnp.int32, (peers, LANES), 1)
    wanted = channel[...] * rsecs + local[...]
    seen = jnp.zeros((peers, LANES), jnp.int32)
    filled = jnp.zeros((peers, LANES), jnp.int32)
    for k in range(blocks):
        hit = peer == owner[:, k : k + 1]
        for j in range(terms):
            filled = jnp.where(hit & (lane == seen * terms + j), wanted[j : j + 1, k : k + 1], filled)
        seen = seen + hit.astype(jnp.int32)
    table[...] = filled[:, : table.shape[1]]


def gather_kernel(table, env, out):
    def fill(p):
        wanted = table[pl.ds(p, 1), :]
        for i in range(table.shape[1]):
            out[p, i * TILES : (i + 1) * TILES, :] = env[wanted[0, i]]

    each(out.shape[0], fill)


def prepare_kernel(
    peers, sector_far, owner_far, couple_far, psi_far, left_far, right_far, right, lcomb, image, wave, slot,
    sector, owner, couple, psi, left_env, right_env, arrived, flat, right_stage, stage, twice,
):
    blocks, terms, chans = couple.shape
    lsecs = left_env.shape[1]
    rsecs = right_env.shape[1]
    wide = flat.shape[0]
    rows = blocks * terms
    moves = [
        pltpu.make_async_copy(source, target, arrived.at[i])
        for i, (source, target) in enumerate(
            (
                (right_far, right_env),
                (left_far, left_env),
                (psi_far, psi),
                (couple_far, couple),
                (sector_far, sector),
                (owner_far, owner),
            )
        )
    ]
    for move in moves:
        move.start()
    flat[chans * lsecs :, :] = jnp.zeros((wide - chans * lsecs, B * B), F32)
    moves[0].wait()

    for w in range(chans):
        slab = right_env[w].astype(F32)
        for t in range(TILES):
            right_stage[pl.ds(w * rsecs * TILES + t, rsecs, stride=TILES), :] = slab[:, t * LANES : (t + 1) * LANES]
    right[...] = right_stage[: chans * rsecs * TILES, :].reshape(right.shape).astype(BF16)

    for move in moves[1:]:
        move.wait()
    own = owner[...]
    lane = lax.broadcasted_iota(jnp.int32, own.shape, 1)
    rank = jnp.zeros_like(own)
    for k in range(blocks):
        rank = rank + ((own == own[:, k : k + 1]) & (lane > k)).astype(jnp.int32)
    slot[...] = replaced(own, [(peer, q) for q, peer in enumerate(ORDER)], peers) * CAP + rank

    is_low = low_half()

    for g in range(blocks // 8):
        waves = psi[g].astype(F32)
        for t in range(TILES):
            tile = waves[:, t * LANES : (t + 1) * LANES]
            base = 8 * g * B + 2 * t
            twice[pl.ds(base, 8, stride=B), :] = jnp.where(is_low, tile, swap(tile))
            twice[pl.ds(base + 1, 8, stride=B), :] = jnp.where(is_low, swap(tile), tile)

    exact = jnp.concatenate([couple[:, j, :] for j in range(terms)], axis=0)
    high = exact.astype(BF16)
    rest = exact - high.astype(F32)
    middle = rest.astype(BF16)
    low = (rest - middle.astype(F32)).astype(BF16)
    column = lax.broadcasted_iota(jnp.int32, (chans, wide), 1)
    begin = lax.broadcasted_iota(jnp.int32, (chans, wide), 0) * lsecs
    spreads = ((column >= begin) & (column < begin + lsecs)).astype(F32).astype(BF16)
    wider = dot(jnp.concatenate([high, middle, low], axis=0), spreads)
    row = lax.broadcasted_iota(jnp.int32, (blocks, wide), 0)
    of_lane = lax.rem(lax.broadcasted_iota(jnp.int32, (blocks, wide), 1), lsecs)
    own_sector = sector[...]
    chosen = jnp.zeros((blocks, wide), jnp.int32)
    for k in range(blocks):
        chosen = jnp.where(row == k, own_sector[:, k : k + 1], chosen)
    mask = (chosen == of_lane).astype(F32)
    parts = (wider * jnp.concatenate([mask] * (3 * terms), axis=0)).astype(BF16)

    for w in range(chans):
        flat[w * lsecs : (w + 1) * lsecs, :] = left_env[w].astype(F32)
    width = 512
    for n in range(B * B // width):
        sums = dot(parts, flat[:, n * width : (n + 1) * width].astype(BF16))
        total = sums[:rows] + (sums[rows : 2 * rows] + sums[2 * rows :])
        for g in range(blocks // 8):
            for t in range(width // LANES):
                lanes = slice(t * LANES, (t + 1) * LANES)
                first = total[8 * g : 8 * g + 8, lanes]
                other = total[blocks + 8 * g : blocks + 8 * g + 8, lanes]
                base = 8 * g * B + 2 * (n * (width // LANES) + t)
                stage[pl.ds(base, 8, stride=B), :] = jnp.where(is_low, first, swap(other))
                stage[pl.ds(base + 1, 8, stride=B), :] = jnp.where(is_low, swap(first), other)

    left_lanes = low_half(B)

    def block(k):
        place = pl.ds(pl.multiple_of(k * B, B), B)
        left = stage[place, :].astype(BF16)
        base = twice[place, :]
        lcomb[k] = left
        wave[k] = base[:, :B]
        both = jnp.concatenate([jnp.where(left_lanes, base, 0.0), jnp.where(left_lanes, 0.0, base)], axis=0)
        image[k] = dot(left, both.astype(BF16)).astype(BF16)

    each(blocks, block)


def fold(values):
    return jnp.sum(values.reshape(B // 8, 8, B), axis=0)


def image_kernel(slot, received, lcomb, image, wave, hpsi, rsel, stats, stage, resid, zed, part):
    blocks = lcomb.shape[0]
    groups = blocks // 8
    places = slot[...]

    for k in range(blocks):
        raw = received[places[0, k]].astype(F32)
        stage[pl.ds(k * 2 * B, B, stride=2), :] = raw
        stage[pl.ds(k * 2 * B + 1, B, stride=2), :] = swap(raw)

    def unfold(k):
        rsel[k] = stage[pl.ds(pl.multiple_of(k * 2 * B, 2 * B), 2 * B), 0:B].astype(BF16)

    each(blocks, unfold)

    def keep(i, k, values):
        part[i, pl.ds(pl.multiple_of(k * 8, 8), 8), :] = fold(values)

    def of_group(i, g):
        sums = part[i, pl.ds(g * 8 * 8, 8, stride=8), :]
        for s in range(1, 8):
            sums = sums + part[i, pl.ds(g * 8 * 8 + s, 8, stride=8), :]
        return jnp.sum(sums, axis=1, keepdims=True)

    def apply(k):
        h = dot(image[k], rsel[k])
        base = wave[k]
        hpsi[k] = h
        keep(0, k, base * base)
        keep(1, k, base * h)

    each(blocks, apply)

    def group(g):
        norm, cross = of_group(0, g), of_group(1, g)
        theta = cross / jnp.maximum(norm, TINY)

        for i in range(8):
            k = g * 8 + i
            h, base = hpsi[k], wave[k]
            rest = h - theta[i : i + 1, :] * base
            resid[k] = rest
            step = rest.astype(BF16)
            zed[k, 0:B] = dot(step, rsel[k, 0:B]).astype(BF16)
            zed[k, B : 2 * B] = dot(step, rsel[k, B : 2 * B]).astype(BF16)
            keep(2, k, rest * rest)
            keep(3, k, rest * base)
            keep(4, k, rest * h)

        for i in range(8):
            k = g * 8 + i
            applied = dot(lcomb[k], zed[k])
            keep(5, k, resid[k] * applied)
            keep(6, k, wave[k] * applied)

        lane = lax.broadcasted_iota(jnp.int32, (8, LANES), 1)
        packed = jnp.zeros((8, LANES), F32)
        for i, value in enumerate([norm, cross] + [of_group(i, g) for i in range(2, STATS)]):
            packed = jnp.where(lane == i, value, packed)
        spread = pltpu.roll(packed, 0, 1, stride=SPACE, stride_axis=0)
        row = jnp.sum(spread, axis=0, keepdims=True)
        if groups == 1:
            stats[...] = jnp.broadcast_to(row, stats.shape)
        else:
            pl.loop(0, stats.shape[0] // groups)(lambda p: stats.__setitem__((pl.ds(p * groups + g, 1), slice(None)), row))

    each(groups, group)


def second_kernel(count, stats, hpsi, wave, rsel, lcomb, second, direction, projected, stage, steps, zed, narrow):
    blocks = lcomb.shape[0]
    held = stats[...]
    here = lax.broadcasted_iota(jnp.int32, held.shape, 1) % SPACE == 0
    norm, cross, square, mixed, image, applied, crossed = (
        jnp.where(here, pltpu.roll(held, (LANES - i) % LANES, 1) if i else held, 0.0) for i in range(STATS)
    )

    def total(values):
        return jnp.sum(jnp.sum(values, axis=0, keepdims=True), axis=1, keepdims=True)

    theta = total(cross) / total(norm)
    shift = theta - cross / jnp.maximum(norm, TINY)
    rr = total(square - 2.0 * shift * mixed + shift * shift * norm)
    along = total(applied - shift * (image + crossed) + shift * shift * cross)
    spread = rr / count
    scale = 1.0 / jnp.sqrt(spread + 1e-06)

    def move(k):
        place = pl.ds(pl.multiple_of(k * B, B), B)
        step = ((hpsi[k] - theta * wave[k]) * scale).astype(BF16)
        narrow[k] = step
        steps[place, 0:B] = step.astype(F32)

    each(blocks, move)

    def apply(k):
        zed[k, 0:B] = dot(narrow[k], rsel[k, 0:B]).astype(BF16)
        zed[k, B : 2 * B] = dot(narrow[k], rsel[k, B : 2 * B]).astype(BF16)

    each(blocks, apply)

    def close(k):
        stage[pl.ds(pl.multiple_of(k * B, B), B), 0:B] = dot(lcomb[k], zed[k])

    each(blocks, close)
    is_low = low_half()

    def rows(g):
        place = pl.ds(pl.multiple_of(8 * g, 8), 8)
        for source, target in ((steps, direction), (stage, second)):
            for t in range(TILES):
                base = 8 * g * B + 2 * t
                even = source[pl.ds(base, 8, stride=B), :]
                odd = source[pl.ds(base + 1, 8, stride=B), :]
                target[place, t * LANES : (t + 1) * LANES] = jnp.where(is_low, even, swap(odd)).astype(target.dtype)

    each(blocks // 8, rows)
    projected[0] = theta[0, 0]
    projected[1] = jnp.sqrt(spread)[0, 0]
    projected[2] = (along / rr)[0, 0]


VMEM = pl.BlockSpec(memory_space=pltpu.VMEM)
SMEM = pl.BlockSpec(memory_space=pltpu.SMEM)


def params(mib):
    return pltpu.CompilerParams(vmem_limit_bytes=mib << 20)


def cost(flops, moved):
    return pl.CostEstimate(flops=flops, bytes_accessed=moved, transcendentals=0)


def per_device(psi, left_env, right_env, couple, left_sector, right_owner, right_local, channel):
    peers = lax.axis_size("sec")
    blocks = psi.shape[0]
    _, terms, chans = couple.shape
    lsecs = left_env.shape[0]
    rsecs = right_env.shape[0]
    slots = peers * CAP
    groups = blocks // 8
    of = jax.ShapeDtypeStruct

    def exchange(values):
        members = [listed(peers)]
        return lax.all_to_all(values, "sec", split_axis=0, concat_axis=0, axis_index_groups=members, tiled=True)

    owner = right_owner.T
    table = pl.pallas_call(
        functools.partial(request_kernel, rsecs),
        out_shape=of((peers, CAP * terms), jnp.int32),
        in_specs=[VMEM] * 3,
        out_specs=VMEM,
        compiler_params=params(4),
        cost_estimate=cost(0, 0),
        name="request",
    )(owner, right_local.reshape(1, blocks), channel.T)
    wanted = exchange(table.reshape(peers, 1, CAP * terms)).reshape(peers, CAP * terms)

    wide = rounded_up(lsecs * chans, LANES)
    inputs = (
        left_sector.reshape(1, blocks),
        owner,
        couple,
        psi.reshape(groups, 8, B * B),
        left_env.transpose(1, 0, 2),
        right_env.transpose(1, 0, 2),
    )
    right, lcomb, image, wave, slot = pl.pallas_call(
        functools.partial(prepare_kernel, peers),
        out_shape=(
            of((chans * rsecs, TILES, LANES), BF16),
            of((blocks, B, terms * B), BF16),
            of((blocks, B, terms * B), BF16),
            of((blocks, B, B), F32),
            of((1, blocks), jnp.int32),
        ),
        in_specs=[pl.BlockSpec(memory_space=pl.ANY)] * len(inputs),
        out_specs=(VMEM,) * 5,
        scratch_shapes=[pltpu.VMEM(x.shape, x.dtype) for x in inputs]
        + [
            pltpu.SemaphoreType.DMA((len(inputs),)),
            pltpu.VMEM((wide, B * B), F32),
            pltpu.VMEM(((chans * rsecs + 1) * TILES, LANES), F32),
            pltpu.VMEM(((blocks + 1) * B, LANES), F32),
            pltpu.VMEM(((blocks + 1) * B, LANES), F32),
        ],
        compiler_params=params(24),
        cost_estimate=cost(100_000_000, 3_000_000),
        name="prepare",
    )(*[pltpu.with_memory_space_constraint(x, pltpu.HBM) for x in inputs])

    sent = pl.pallas_call(
        gather_kernel,
        out_shape=of((peers, CAP * terms * TILES, LANES), BF16),
        in_specs=[VMEM, VMEM],
        out_specs=VMEM,
        compiler_params=params(8),
        name="gather",
    )(wanted, right)
    received = exchange(sent).reshape(slots, terms * TILES, LANES)

    hpsi, rsel, stats = pl.pallas_call(
        image_kernel,
        out_shape=(
            of((blocks, B, B), F32),
            of((blocks, terms * B, B), BF16),
            of((peers * groups, LANES), F32),
        ),
        in_specs=[VMEM] * 5,
        out_specs=(VMEM, VMEM, VMEM),
        scratch_shapes=[
            pltpu.VMEM(((blocks * terms + 1) * B, LANES), F32),
            pltpu.VMEM((blocks, B, B), F32),
            pltpu.VMEM((blocks, terms * B, B), BF16),
            pltpu.VMEM((STATS, (blocks + 1) * 8, B), F32),
        ],
        compiler_params=params(24),
        name="image",
    )(slot, received, lcomb, image, wave)
    stats = exchange(stats.reshape(peers, groups, LANES)).reshape(peers * groups, LANES)

    second, direction, projected = pl.pallas_call(
        functools.partial(second_kernel, float(blocks * peers * B * B)),
        out_shape=(of((blocks, B * B), F32), of((blocks, B * B), BF16), of((3,), F32)),
        in_specs=[VMEM] * 5,
        out_specs=(VMEM, VMEM, SMEM),
        scratch_shapes=[
            pltpu.VMEM(((blocks + 1) * B, LANES), F32),
            pltpu.VMEM(((blocks + 1) * B, LANES), F32),
            pltpu.VMEM((blocks, terms * B, B), BF16),
            pltpu.VMEM((blocks, B, B), BF16),
        ],
        compiler_params=params(24),
        name="second",
    )(stats, hpsi, wave, rsel, lcomb)
    return second, direction, projected


def solution(mesh):
    placed = (
        P(("parts", "sec"), None),
        P(("parts", "sec"), None, None),
        P(("parts", "sec"), None, None),
        P(("parts", "sec"), None, None),
        P(("parts", "sec")),
        P(("parts", "sec"), None),
        P(("parts", "sec")),
        P(("parts", "sec"), None),
    )
    return jax.shard_map(
        per_device,
        mesh=mesh,
        in_specs=placed,
        out_specs=(P(("parts", "sec"), None), P(("parts", "sec"), None), P("parts")),
        check_vma=False,
    )
```

```python
import functools

import jax
import jax.numpy as jnp
from jax import lax
from jax.experimental import pallas as pl
from jax.experimental.pallas import tpu as pltpu
from jax.sharding import PartitionSpec as P

B = 64
CAP = 2
LANES = 128
TILES = B * B // LANES
STATS = 5
SPACE = 16
TINY = 1e-30
ORDER = (11, 2, 14, 6, 9, 7, 13, 10, 8, 5, 4, 12, 1, 15, 0, 3)
F32 = jnp.float32
BF16 = jnp.bfloat16


def rounded_up(value, step):
    return -(-value // step) * step


def each(count, body):
    if count <= 32:
        for i in range(count):
            body(i)
    else:
        pl.loop(0, count)(body)


def run_of(peers):
    return 0 if peers % len(ORDER) else peers // len(ORDER)


def listed(peers):
    run = run_of(peers)
    return [q * run + i for q in ORDER for i in range(run)] if run else list(range(peers))


def replaced(values, pairs, peers):
    run = run_of(peers)
    if not run:
        return values
    whole = values // run if run > 1 else values
    moved = values
    for old, new in pairs:
        moved = jnp.where(whole == old, values + (new - old) * run, moved)
    return moved


def dot(a, b):
    return jnp.dot(a, b, preferred_element_type=F32)


def summed(values):
    return jnp.sum(jnp.sum(values, axis=0, keepdims=True), axis=1, keepdims=True)


def low_half(rows=8):
    return lax.broadcasted_iota(jnp.int32, (rows, LANES), 1) < B


def swap(tile):
    return pltpu.roll(tile, B, 1)


def request_kernel(rsecs, owner, local, channel, table):
    terms, blocks = channel.shape
    peers = table.shape[0]
    peer = lax.broadcasted_iota(jnp.int32, (peers, LANES), 0)
    peer = replaced(peer, enumerate(ORDER), peers)
    lane = lax.broadcasted_iota(jnp.int32, (peers, LANES), 1)
    wanted = channel[...] * rsecs + local[...]
    seen = jnp.zeros((peers, LANES), jnp.int32)
    filled = jnp.zeros((peers, LANES), jnp.int32)
    for k in range(blocks):
        hit = peer == owner[:, k : k + 1]
        for j in range(terms):
            filled = jnp.where(hit & (lane == seen * terms + j), wanted[j : j + 1, k : k + 1], filled)
        seen = seen + hit.astype(jnp.int32)
    table[...] = filled[:, : table.shape[1]]


def gather_kernel(table, env, out):
    def fill(p):
        wanted = table[pl.ds(p, 1), :]
        for i in range(table.shape[1]):
            out[p, i * TILES : (i + 1) * TILES, :] = env[wanted[0, i]]

    each(out.shape[0], fill)


def prepare_kernel(
    peers, sector_far, owner_far, couple_far, psi_far, left_far, right_far, right, lcomb, image, wave, norm, slot,
    sector, owner, couple, psi, left_env, right_env, arrived, flat, right_stage, stage, twice,
):
    blocks, terms, chans = couple.shape
    lsecs = left_env.shape[1]
    rsecs = right_env.shape[1]
    wide = flat.shape[0]
    rows = blocks * terms
    moves = [
        pltpu.make_async_copy(source, target, arrived.at[i])
        for i, (source, target) in enumerate(
            (
                (right_far, right_env),
                (left_far, left_env),
                (psi_far, psi),
                (couple_far, couple),
                (sector_far, sector),
                (owner_far, owner),
            )
        )
    ]
    for move in moves:
        move.start()
    flat[chans * lsecs :, :] = jnp.zeros((wide - chans * lsecs, B * B), F32)
    moves[0].wait()

    for w in range(chans):
        slab = right_env[w].astype(F32)
        for t in range(TILES):
            right_stage[pl.ds(w * rsecs * TILES + t, rsecs, stride=TILES), :] = slab[:, t * LANES : (t + 1) * LANES]
    right[...] = right_stage[: chans * rsecs * TILES, :].reshape(right.shape).astype(BF16)

    for move in moves[1:]:
        move.wait()
    own = owner[...]
    lane = lax.broadcasted_iota(jnp.int32, own.shape, 1)
    rank = jnp.zeros_like(own)
    for k in range(blocks):
        rank = rank + ((own == own[:, k : k + 1]) & (lane > k)).astype(jnp.int32)
    slot[...] = replaced(own, [(peer, q) for q, peer in enumerate(ORDER)], peers) * CAP + rank

    is_low = low_half()

    for g in range(blocks // 8):
        waves = psi[g].astype(F32)
        for t in range(TILES):
            tile = waves[:, t * LANES : (t + 1) * LANES]
            base = 8 * g * B + t
            twice[pl.ds(base, 8, stride=B), :] = jnp.where(is_low, tile, swap(tile))
            twice[pl.ds(base + TILES, 8, stride=B), :] = jnp.where(is_low, swap(tile), tile)

    exact = jnp.concatenate([couple[:, j, :] for j in range(terms)], axis=0)
    high = exact.astype(BF16)
    rest = exact - high.astype(F32)
    middle = rest.astype(BF16)
    low = (rest - middle.astype(F32)).astype(BF16)
    column = lax.broadcasted_iota(jnp.int32, (chans, wide), 1)
    begin = lax.broadcasted_iota(jnp.int32, (chans, wide), 0) * lsecs
    spreads = ((column >= begin) & (column < begin + lsecs)).astype(F32).astype(BF16)
    wider = dot(jnp.concatenate([high, middle, low], axis=0), spreads)
    row = lax.broadcasted_iota(jnp.int32, (blocks, wide), 0)
    of_lane = lax.rem(lax.broadcasted_iota(jnp.int32, (blocks, wide), 1), lsecs)
    own_sector = sector[...]
    chosen = jnp.zeros((blocks, wide), jnp.int32)
    for k in range(blocks):
        chosen = jnp.where(row == k, own_sector[:, k : k + 1], chosen)
    mask = (chosen == of_lane).astype(F32)
    parts = (wider * jnp.concatenate([mask] * (3 * terms), axis=0)).astype(BF16)

    for w in range(chans):
        flat[w * lsecs : (w + 1) * lsecs, :] = left_env[w].astype(F32)
    width = 512
    for n in range(B * B // width):
        sums = dot(parts, flat[:, n * width : (n + 1) * width].astype(BF16))
        total = sums[:rows] + (sums[rows : 2 * rows] + sums[2 * rows :])
        for g in range(blocks // 8):
            for t in range(width // LANES):
                lanes = slice(t * LANES, (t + 1) * LANES)
                first = total[8 * g : 8 * g + 8, lanes]
                other = total[blocks + 8 * g : blocks + 8 * g + 8, lanes]
                base = 8 * g * B + n * (width // LANES) + t
                stage[pl.ds(base, 8, stride=B), :] = jnp.where(is_low, first, swap(other))
                stage[pl.ds(base + TILES, 8, stride=B), :] = jnp.where(is_low, swap(first), other)

    left_lanes = low_half(B)
    column = lax.broadcasted_iota(jnp.int32, (LANES, LANES), 0)
    within = column & (B - 1)
    moved = column - within + (within & 1) * TILES + (within >> 1)
    order = (lax.broadcasted_iota(jnp.int32, (LANES, LANES), 1) == moved).astype(F32).astype(BF16)

    def block(k):
        place = pl.ds(pl.multiple_of(k * B, B), B)
        left = dot(stage[place, :].astype(BF16), order).astype(BF16)
        base = twice[place, :]
        lcomb[k] = left
        wave[k] = base
        norm[pl.ds(k, 1), :] = summed(base[:, :B] * base[:, :B])
        both = jnp.concatenate([jnp.where(left_lanes, base, 0.0), jnp.where(left_lanes, 0.0, base)], axis=0)
        image[k] = dot(left, both.astype(BF16)).astype(BF16)

    each(blocks, block)


def fold(values):
    return jnp.sum(values[:, :B].reshape(B // 8, 8, B), axis=0)


def packed_rows(values):
    return jnp.where(low_half(TILES), values[:TILES], values[TILES:])


def image_kernel(slot, norm, received, lcomb, image, wave, hpsi, rsel, stats, stage, resid, zed, part):
    blocks = lcomb.shape[0]
    groups = blocks // 8
    places = slot[...]
    is_low = low_half(B)

    for k in range(blocks):
        raw = received[places[0, k]].astype(F32)
        turned = swap(raw)
        stage[pl.ds(k * 2 * B, B, stride=2), :] = jnp.where(is_low, raw, turned)
        stage[pl.ds(k * 2 * B + 1, B, stride=2), :] = jnp.where(is_low, turned, raw)

    def unfold(k):
        rsel[k] = stage[pl.ds(pl.multiple_of(k * 2 * B, 2 * B), 2 * B), :].astype(BF16)

    each(blocks, unfold)

    def keep(i, k, values):
        part[i, pl.ds(pl.multiple_of(k * 8, 8), 8), :] = fold(values)

    def of_group(i, g):
        sums = part[i, pl.ds(g * 8 * 8, 8, stride=8), :]
        for s in range(1, 8):
            sums = sums + part[i, pl.ds(g * 8 * 8 + s, 8, stride=8), :]
        return jnp.sum(sums, axis=1, keepdims=True)

    def apply(k):
        h = dot(image[k], rsel[k])
        hpsi[k] = h
        keep(0, k, wave[k] * h)

    each(blocks, apply)

    def group(g):
        own_norm, cross = norm[pl.ds(g * 8, 8), :], of_group(0, g)
        theta = cross / jnp.maximum(own_norm, TINY)

        for i in range(8):
            k = g * 8 + i
            h, base = hpsi[k], wave[k]
            rest = h - theta[i : i + 1, :] * base
            resid[k] = rest
            step = rest[:, :B].astype(BF16)
            zed[k, 0:B] = dot(step, rsel[k, 0:B]).astype(BF16)
            zed[k, B : 2 * B] = dot(step, rsel[k, B : 2 * B]).astype(BF16)
            keep(1, k, rest * rest)

        for i in range(8):
            k = g * 8 + i
            applied = dot(lcomb[k], zed[k])
            keep(2, k, resid[k] * applied)
            keep(3, k, wave[k] * applied)

        lane = lax.broadcasted_iota(jnp.int32, (8, LANES), 1)
        packed = jnp.zeros((8, LANES), F32)
        for i, value in enumerate([own_norm, cross] + [of_group(i, g) for i in range(1, STATS - 1)]):
            packed = jnp.where(lane == i, value, packed)
        spread = pltpu.roll(packed, 0, 1, stride=SPACE, stride_axis=0)
        row = jnp.sum(spread, axis=0, keepdims=True)
        if groups == 1:
            stats[...] = jnp.broadcast_to(row, stats.shape)
        else:
            pl.loop(0, stats.shape[0] // groups)(lambda p: stats.__setitem__((pl.ds(p * groups + g, 1), slice(None)), row))

    each(groups, group)


def second_kernel(count, stats, hpsi, wave, rsel, lcomb, second, direction, projected, stage, steps, zed, narrow):
    blocks = lcomb.shape[0]
    held = stats[...]
    here = lax.broadcasted_iota(jnp.int32, held.shape, 1) % SPACE == 0
    norm, cross, square, applied, crossed = (
        jnp.where(here, pltpu.roll(held, (LANES - i) % LANES, 1) if i else held, 0.0) for i in range(STATS)
    )

    theta = summed(cross) / summed(norm)
    own = cross / jnp.maximum(norm, TINY)
    mixed = cross - own * norm
    image = square + own * mixed
    shift = theta - own
    rr = summed(square - 2.0 * shift * mixed + shift * shift * norm)
    along = summed(applied - shift * (image + crossed) + shift * shift * cross)
    spread = rr / count
    scale = 1.0 / jnp.sqrt(spread + 1e-06)

    def rows_of(k):
        return pl.ds(k // 8 * (8 * TILES) + k % 8, TILES, stride=8)

    def move(k):
        step = ((hpsi[k] - theta * wave[k]) * scale).astype(BF16)
        narrow[k] = step[:, :B]
        steps[rows_of(k), :] = packed_rows(step.astype(F32))

    each(blocks, move)

    def apply(k):
        zed[k, 0:B] = dot(narrow[k], rsel[k, 0:B]).astype(BF16)
        zed[k, B : 2 * B] = dot(narrow[k], rsel[k, B : 2 * B]).astype(BF16)

    each(blocks, apply)

    def close(k):
        stage[rows_of(k), :] = packed_rows(dot(lcomb[k], zed[k]))

    each(blocks, close)

    def rows(g):
        place = pl.ds(pl.multiple_of(8 * g, 8), 8)
        for source, target in ((steps, direction), (stage, second)):
            for t in range(TILES):
                tile = source[pl.ds(pl.multiple_of((g * TILES + t) * 8, 8), 8), :]
                target[place, t * LANES : (t + 1) * LANES] = tile.astype(target.dtype)

    each(blocks // 8, rows)
    projected[0] = theta[0, 0]
    projected[1] = jnp.sqrt(spread)[0, 0]
    projected[2] = (along / rr)[0, 0]


VMEM = pl.BlockSpec(memory_space=pltpu.VMEM)
SMEM = pl.BlockSpec(memory_space=pltpu.SMEM)


def params(mib):
    return pltpu.CompilerParams(vmem_limit_bytes=mib << 20)


def cost(flops, moved):
    return pl.CostEstimate(flops=flops, bytes_accessed=moved, transcendentals=0)


def per_device(psi, left_env, right_env, couple, left_sector, right_owner, right_local, channel):
    peers = lax.axis_size("sec")
    blocks = psi.shape[0]
    _, terms, chans = couple.shape
    lsecs = left_env.shape[0]
    rsecs = right_env.shape[0]
    slots = peers * CAP
    groups = blocks // 8
    of = jax.ShapeDtypeStruct

    def exchange(values):
        members = [listed(peers)]
        return lax.all_to_all(values, "sec", split_axis=0, concat_axis=0, axis_index_groups=members, tiled=True)

    owner = right_owner.T
    table = pl.pallas_call(
        functools.partial(request_kernel, rsecs),
        out_shape=of((peers, CAP * terms), jnp.int32),
        in_specs=[VMEM] * 3,
        out_specs=VMEM,
        compiler_params=params(4),
        cost_estimate=cost(0, 0),
        name="request",
    )(owner, right_local.reshape(1, blocks), channel.T)
    wanted = exchange(table.reshape(peers, 1, CAP * terms)).reshape(peers, CAP * terms)

    wide = rounded_up(lsecs * chans, LANES)
    inputs = (
        left_sector.reshape(1, blocks),
        owner,
        couple,
        psi.reshape(groups, 8, B * B),
        left_env.transpose(1, 0, 2),
        right_env.transpose(1, 0, 2),
    )
    right, lcomb, image, wave, norm, slot = pl.pallas_call(
        functools.partial(prepare_kernel, peers),
        out_shape=(
            of((chans * rsecs, TILES, LANES), BF16),
            of((blocks, B, terms * B), BF16),
            of((blocks, B, terms * B), BF16),
            of((blocks, B, LANES), F32),
            of((blocks, 1), F32),
            of((1, blocks), jnp.int32),
        ),
        in_specs=[pl.BlockSpec(memory_space=pl.ANY)] * len(inputs),
        out_specs=(VMEM,) * 6,
        scratch_shapes=[pltpu.VMEM(x.shape, x.dtype) for x in inputs]
        + [
            pltpu.SemaphoreType.DMA((len(inputs),)),
            pltpu.VMEM((wide, B * B), F32),
            pltpu.VMEM(((chans * rsecs + 1) * TILES, LANES), F32),
            pltpu.VMEM(((blocks + 1) * B, LANES), F32),
            pltpu.VMEM(((blocks + 1) * B, LANES), F32),
        ],
        compiler_params=params(24),
        cost_estimate=cost(100_000_000, 3_000_000),
        name="prepare",
    )(*[pltpu.with_memory_space_constraint(x, pltpu.HBM) for x in inputs])

    sent = pl.pallas_call(
        gather_kernel,
        out_shape=of((peers, CAP * terms * TILES, LANES), BF16),
        in_specs=[VMEM, VMEM],
        out_specs=VMEM,
        compiler_params=params(8),
        name="gather",
    )(wanted, right)
    received = exchange(sent).reshape(slots, terms * TILES, LANES)

    hpsi, rsel, stats = pl.pallas_call(
        image_kernel,
        out_shape=(
            of((blocks, B, LANES), F32),
            of((blocks, terms * B, LANES), BF16),
            of((peers * groups, LANES), F32),
        ),
        in_specs=[VMEM] * 6,
        out_specs=(VMEM, VMEM, VMEM),
        scratch_shapes=[
            pltpu.VMEM(((blocks * terms + 1) * B, LANES), F32),
            pltpu.VMEM((blocks, B, LANES), F32),
            pltpu.VMEM((blocks, terms * B, LANES), BF16),
            pltpu.VMEM((STATS - 1, (blocks + 1) * 8, B), F32),
        ],
        compiler_params=params(24),
        name="image",
    )(slot, norm, received, lcomb, image, wave)
    stats = exchange(stats.reshape(peers, groups, LANES)).reshape(peers * groups, LANES)

    second, direction, projected = pl.pallas_call(
        functools.partial(second_kernel, float(blocks * peers * B * B)),
        out_shape=(of((blocks, B * B), F32), of((blocks, B * B), BF16), of((3,), F32)),
        in_specs=[VMEM] * 5,
        out_specs=(VMEM, VMEM, SMEM),
        scratch_shapes=[
            pltpu.VMEM((blocks * TILES + 8, LANES), F32),
            pltpu.VMEM((blocks * TILES + 8, LANES), F32),
            pltpu.VMEM((blocks, terms * B, LANES), BF16),
            pltpu.VMEM((blocks, B, B), BF16),
        ],
        compiler_params=params(24),
        name="second",
    )(stats, hpsi, wave, rsel, lcomb)
    return second, direction, projected


def solution(mesh):
    placed = (
        P(("parts", "sec"), None),
        P(("parts", "sec"), None, None),
        P(("parts", "sec"), None, None),
        P(("parts", "sec"), None, None),
        P(("parts", "sec")),
        P(("parts", "sec"), None),
        P(("parts", "sec")),
        P(("parts", "sec"), None),
    )
    return jax.shard_map(
        per_device,
        mesh=mesh,
        in_specs=placed,
        out_specs=(P(("parts", "sec"), None), P(("parts", "sec"), None), P("parts")),
        check_vma=False,
    )
```

```python
import functools

import jax
import jax.numpy as jnp
from jax import lax
from jax.experimental import pallas as pl
from jax.experimental.pallas import tpu as pltpu
from jax.sharding import PartitionSpec as P

B = 64
CAP = 2
LANES = 128
TILES = B * B // LANES
STATS = 5
SPACE = 16
TINY = 1e-30
ORDER = (11, 13, 15, 1, 2, 3, 7, 14, 6, 9, 5, 12, 8, 4, 10, 0)
F32 = jnp.float32
BF16 = jnp.bfloat16


def rounded_up(value, step):
    return -(-value // step) * step


def each(count, body):
    if count <= 32:
        for i in range(count):
            body(i)
    else:
        pl.loop(0, count)(body)


def run_of(peers):
    return 0 if peers % len(ORDER) else peers // len(ORDER)


def listed(peers):
    run = run_of(peers)
    return [q * run + i for q in ORDER for i in range(run)] if run else list(range(peers))


def replaced(values, pairs, peers):
    run = run_of(peers)
    if not run:
        return values
    whole = values // run if run > 1 else values
    moved = values
    for old, new in pairs:
        moved = jnp.where(whole == old, values + (new - old) * run, moved)
    return moved


def dot(a, b):
    return jnp.dot(a, b, preferred_element_type=F32)


def summed(values):
    return jnp.sum(jnp.sum(values, axis=0, keepdims=True), axis=1, keepdims=True)


def low_half(rows=8):
    return lax.broadcasted_iota(jnp.int32, (rows, LANES), 1) < B


def swap(tile):
    return pltpu.roll(tile, B, 1)


def request_kernel(rsecs, owner, local, channel, table):
    terms, blocks = channel.shape
    peers = table.shape[0]
    peer = lax.broadcasted_iota(jnp.int32, (peers, LANES), 0)
    peer = replaced(peer, enumerate(ORDER), peers)
    lane = lax.broadcasted_iota(jnp.int32, (peers, LANES), 1)
    wanted = channel[...] * rsecs + local[...]
    seen = jnp.zeros((peers, LANES), jnp.int32)
    filled = jnp.zeros((peers, LANES), jnp.int32)
    for k in range(blocks):
        hit = peer == owner[:, k : k + 1]
        for j in range(terms):
            filled = jnp.where(hit & (lane == seen * terms + j), wanted[j : j + 1, k : k + 1], filled)
        seen = seen + hit.astype(jnp.int32)
    table[...] = filled[:, : table.shape[1]]


def gather_kernel(table, env, out):
    def fill(p):
        wanted = table[pl.ds(p, 1), :]
        for i in range(table.shape[1]):
            out[p, i * TILES : (i + 1) * TILES, :] = env[wanted[0, i]]

    each(out.shape[0], fill)


def prepare_kernel(
    peers, sector_far, owner_far, couple_far, psi_far, left_far, right_far, right, lcomb, image, wave, norm, slot,
    sector, owner, couple, psi, left_env, right_env, arrived, flat, right_stage, stage, twice,
):
    blocks, terms, chans = couple.shape
    lsecs = left_env.shape[1]
    rsecs = right_env.shape[1]
    wide = flat.shape[0]
    rows = blocks * terms
    moves = [
        pltpu.make_async_copy(source, target, arrived.at[i])
        for i, (source, target) in enumerate(
            (
                (right_far, right_env),
                (left_far, left_env),
                (psi_far, psi),
                (couple_far, couple),
                (sector_far, sector),
                (owner_far, owner),
            )
        )
    ]
    for move in moves:
        move.start()
    flat[chans * lsecs :, :] = jnp.zeros((wide - chans * lsecs, B * B), F32)
    moves[0].wait()

    for w in range(chans):
        slab = right_env[w].astype(F32)
        for t in range(TILES):
            right_stage[pl.ds(w * rsecs * TILES + t, rsecs, stride=TILES), :] = slab[:, t * LANES : (t + 1) * LANES]
    right[...] = right_stage[: chans * rsecs * TILES, :].reshape(right.shape).astype(BF16)

    for move in moves[1:]:
        move.wait()
    own = owner[...]
    lane = lax.broadcasted_iota(jnp.int32, own.shape, 1)
    rank = jnp.zeros_like(own)
    for k in range(blocks):
        rank = rank + ((own == own[:, k : k + 1]) & (lane > k)).astype(jnp.int32)
    slot[...] = replaced(own, [(peer, q) for q, peer in enumerate(ORDER)], peers) * CAP + rank

    is_low = low_half()

    for g in range(blocks // 8):
        waves = psi[g].astype(F32)
        for t in range(TILES):
            tile = waves[:, t * LANES : (t + 1) * LANES]
            base = 8 * g * B + t
            twice[pl.ds(base, 8, stride=B), :] = jnp.where(is_low, tile, swap(tile))
            twice[pl.ds(base + TILES, 8, stride=B), :] = jnp.where(is_low, swap(tile), tile)

    exact = jnp.concatenate([couple[:, j, :] for j in range(terms)], axis=0)
    high = exact.astype(BF16)
    rest = exact - high.astype(F32)
    middle = rest.astype(BF16)
    low = (rest - middle.astype(F32)).astype(BF16)
    column = lax.broadcasted_iota(jnp.int32, (chans, wide), 1)
    begin = lax.broadcasted_iota(jnp.int32, (chans, wide), 0) * lsecs
    spreads = ((column >= begin) & (column < begin + lsecs)).astype(F32).astype(BF16)
    wider = dot(jnp.concatenate([high, middle, low], axis=0), spreads)
    row = lax.broadcasted_iota(jnp.int32, (blocks, wide), 0)
    of_lane = lax.rem(lax.broadcasted_iota(jnp.int32, (blocks, wide), 1), lsecs)
    own_sector = sector[...]
    chosen = jnp.zeros((blocks, wide), jnp.int32)
    for k in range(blocks):
        chosen = jnp.where(row == k, own_sector[:, k : k + 1], chosen)
    mask = (chosen == of_lane).astype(F32)
    parts = (wider * jnp.concatenate([mask] * (3 * terms), axis=0)).astype(BF16)

    for w in range(chans):
        flat[w * lsecs : (w + 1) * lsecs, :] = left_env[w].astype(F32)
    width = 512
    for n in range(B * B // width):
        sums = dot(parts, flat[:, n * width : (n + 1) * width].astype(BF16))
        total = sums[:rows] + (sums[rows : 2 * rows] + sums[2 * rows :])
        for g in range(blocks // 8):
            for t in range(width // LANES):
                lanes = slice(t * LANES, (t + 1) * LANES)
                first = total[8 * g : 8 * g + 8, lanes]
                other = total[blocks + 8 * g : blocks + 8 * g + 8, lanes]
                base = 8 * g * B + n * (width // LANES) + t
                stage[pl.ds(base, 8, stride=B), :] = jnp.where(is_low, first, swap(other))
                stage[pl.ds(base + TILES, 8, stride=B), :] = jnp.where(is_low, swap(first), other)

    left_lanes = low_half(B)
    column = lax.broadcasted_iota(jnp.int32, (LANES, LANES), 0)
    within = column & (B - 1)
    moved = column - within + (within & 1) * TILES + (within >> 1)
    order = (lax.broadcasted_iota(jnp.int32, (LANES, LANES), 1) == moved).astype(F32).astype(BF16)

    def block(k):
        place = pl.ds(pl.multiple_of(k * B, B), B)
        left = dot(stage[place, :].astype(BF16), order).astype(BF16)
        base = twice[place, :]
        lcomb[k] = left
        wave[k] = base
        norm[pl.ds(k, 1), :] = summed(base[:, :B] * base[:, :B])
        both = jnp.concatenate([jnp.where(left_lanes, base, 0.0), jnp.where(left_lanes, 0.0, base)], axis=0)
        image[k] = dot(left, both.astype(BF16)).astype(BF16)

    each(blocks, block)


def fold(values):
    return jnp.sum(values[:, :B].reshape(B // 8, 8, B), axis=0)


def packed_rows(values):
    return jnp.where(low_half(TILES), values[:TILES], values[TILES:])


def image_kernel(slot, norm, received, lcomb, image, wave, hpsi, rsel, stats, stage, resid, zed, part):
    blocks = lcomb.shape[0]
    groups = blocks // 8
    places = slot[...]
    is_low = low_half(B)

    for k in range(blocks):
        raw = received[places[0, k]].astype(F32)
        turned = swap(raw)
        stage[pl.ds(k * 2 * B, B, stride=2), :] = jnp.where(is_low, raw, turned)
        stage[pl.ds(k * 2 * B + 1, B, stride=2), :] = jnp.where(is_low, turned, raw)

    def unfold(k):
        rsel[k] = stage[pl.ds(pl.multiple_of(k * 2 * B, 2 * B), 2 * B), :].astype(BF16)

    each(blocks, unfold)

    def keep(i, k, values):
        part[i, pl.ds(pl.multiple_of(k * 8, 8), 8), :] = fold(values)

    def of_group(i, g):
        sums = part[i, pl.ds(g * 8 * 8, 8, stride=8), :]
        for s in range(1, 8):
            sums = sums + part[i, pl.ds(g * 8 * 8 + s, 8, stride=8), :]
        return jnp.sum(sums, axis=1, keepdims=True)

    def apply(k):
        h = dot(image[k], rsel[k])
        hpsi[k] = h
        keep(0, k, wave[k] * h)

    each(blocks, apply)

    def group(g):
        own_norm, cross = norm[pl.ds(g * 8, 8), :], of_group(0, g)
        theta = cross / jnp.maximum(own_norm, TINY)

        for i in range(8):
            k = g * 8 + i
            h, base = hpsi[k], wave[k]
            rest = h - theta[i : i + 1, :] * base
            resid[k] = rest
            step = rest[:, :B].astype(BF16)
            zed[k, 0:B] = dot(step, rsel[k, 0:B]).astype(BF16)
            zed[k, B : 2 * B] = dot(step, rsel[k, B : 2 * B]).astype(BF16)
            keep(1, k, rest * rest)

        for i in range(8):
            k = g * 8 + i
            applied = dot(lcomb[k], zed[k])
            keep(2, k, resid[k] * applied)
            keep(3, k, wave[k] * applied)

        lane = lax.broadcasted_iota(jnp.int32, (8, LANES), 1)
        packed = jnp.zeros((8, LANES), F32)
        for i, value in enumerate([own_norm, cross] + [of_group(i, g) for i in range(1, STATS - 1)]):
            packed = jnp.where(lane == i, value, packed)
        spread = pltpu.roll(packed, 0, 1, stride=SPACE, stride_axis=0)
        row = jnp.sum(spread, axis=0, keepdims=True)
        if groups == 1:
            stats[...] = jnp.broadcast_to(row, stats.shape)
        else:
            pl.loop(0, stats.shape[0] // groups)(lambda p: stats.__setitem__((pl.ds(p * groups + g, 1), slice(None)), row))

    each(groups, group)


def second_kernel(count, stats, hpsi, wave, rsel, lcomb, second, direction, projected, stage, steps, zed, narrow):
    blocks = lcomb.shape[0]
    held = stats[...]
    here = lax.broadcasted_iota(jnp.int32, held.shape, 1) % SPACE == 0
    norm, cross, square, applied, crossed = (
        jnp.where(here, pltpu.roll(held, (LANES - i) % LANES, 1) if i else held, 0.0) for i in range(STATS)
    )

    theta = summed(cross) / summed(norm)
    own = cross / jnp.maximum(norm, TINY)
    mixed = cross - own * norm
    image = square + own * mixed
    shift = theta - own
    rr = summed(square - 2.0 * shift * mixed + shift * shift * norm)
    along = summed(applied - shift * (image + crossed) + shift * shift * cross)
    spread = rr / count
    scale = 1.0 / jnp.sqrt(spread + 1e-06)

    def rows_of(k):
        return pl.ds(k // 8 * (8 * TILES) + k % 8, TILES, stride=8)

    def move(k):
        step = ((hpsi[k] - theta * wave[k]) * scale).astype(BF16)
        narrow[k] = step[:, :B]
        steps[rows_of(k), :] = packed_rows(step.astype(F32))

    each(blocks, move)

    def apply(k):
        zed[k, 0:B] = dot(narrow[k], rsel[k, 0:B]).astype(BF16)
        zed[k, B : 2 * B] = dot(narrow[k], rsel[k, B : 2 * B]).astype(BF16)

    each(blocks, apply)

    def close(k):
        stage[rows_of(k), :] = packed_rows(dot(lcomb[k], zed[k]))

    each(blocks, close)

    def rows(g):
        place = pl.ds(pl.multiple_of(8 * g, 8), 8)
        for source, target in ((steps, direction), (stage, second)):
            for t in range(TILES):
                tile = source[pl.ds(pl.multiple_of((g * TILES + t) * 8, 8), 8), :]
                target[place, t * LANES : (t + 1) * LANES] = tile.astype(target.dtype)

    each(blocks // 8, rows)
    projected[0] = theta[0, 0]
    projected[1] = jnp.sqrt(spread)[0, 0]
    projected[2] = (along / rr)[0, 0]


VMEM = pl.BlockSpec(memory_space=pltpu.VMEM)
SMEM = pl.BlockSpec(memory_space=pltpu.SMEM)


def params(mib):
    return pltpu.CompilerParams(vmem_limit_bytes=mib << 20)


def cost(flops, moved):
    return pl.CostEstimate(flops=flops, bytes_accessed=moved, transcendentals=0)


def per_device(psi, left_env, right_env, couple, left_sector, right_owner, right_local, channel):
    peers = lax.axis_size("sec")
    blocks = psi.shape[0]
    _, terms, chans = couple.shape
    lsecs = left_env.shape[0]
    rsecs = right_env.shape[0]
    slots = peers * CAP
    groups = blocks // 8
    of = jax.ShapeDtypeStruct

    def exchange(values):
        members = [listed(peers)]
        return lax.all_to_all(values, "sec", split_axis=0, concat_axis=0, axis_index_groups=members, tiled=True)

    owner = right_owner.T
    table = pl.pallas_call(
        functools.partial(request_kernel, rsecs),
        out_shape=of((peers, CAP * terms), jnp.int32),
        in_specs=[VMEM] * 3,
        out_specs=VMEM,
        compiler_params=params(4),
        cost_estimate=cost(0, 0),
        name="request",
    )(owner, right_local.reshape(1, blocks), channel.T)
    wanted = exchange(table.reshape(peers, 1, CAP * terms)).reshape(peers, CAP * terms)

    wide = rounded_up(lsecs * chans, LANES)
    inputs = (
        left_sector.reshape(1, blocks),
        owner,
        couple,
        psi.reshape(groups, 8, B * B),
        left_env.transpose(1, 0, 2),
        right_env.transpose(1, 0, 2),
    )
    right, lcomb, image, wave, norm, slot = pl.pallas_call(
        functools.partial(prepare_kernel, peers),
        out_shape=(
            of((chans * rsecs, TILES, LANES), BF16),
            of((blocks, B, terms * B), BF16),
            of((blocks, B, terms * B), BF16),
            of((blocks, B, LANES), F32),
            of((blocks, 1), F32),
            of((1, blocks), jnp.int32),
        ),
        in_specs=[pl.BlockSpec(memory_space=pl.ANY)] * len(inputs),
        out_specs=(VMEM,) * 6,
        scratch_shapes=[pltpu.VMEM(x.shape, x.dtype) for x in inputs]
        + [
            pltpu.SemaphoreType.DMA((len(inputs),)),
            pltpu.VMEM((wide, B * B), F32),
            pltpu.VMEM(((chans * rsecs + 1) * TILES, LANES), F32),
            pltpu.VMEM(((blocks + 1) * B, LANES), F32),
            pltpu.VMEM(((blocks + 1) * B, LANES), F32),
        ],
        compiler_params=params(24),
        cost_estimate=cost(100_000_000, 3_000_000),
        name="prepare",
    )(*[pltpu.with_memory_space_constraint(x, pltpu.HBM) for x in inputs])

    sent = pl.pallas_call(
        gather_kernel,
        out_shape=of((peers, CAP * terms * TILES, LANES), BF16),
        in_specs=[VMEM, VMEM],
        out_specs=VMEM,
        compiler_params=params(8),
        name="gather",
    )(wanted, right)
    received = exchange(sent).reshape(slots, terms * TILES, LANES)

    hpsi, rsel, stats = pl.pallas_call(
        image_kernel,
        out_shape=(
            of((blocks, B, LANES), F32),
            of((blocks, terms * B, LANES), BF16),
            of((peers * groups, LANES), F32),
        ),
        in_specs=[VMEM] * 6,
        out_specs=(VMEM, VMEM, VMEM),
        scratch_shapes=[
            pltpu.VMEM(((blocks * terms + 1) * B, LANES), F32),
            pltpu.VMEM((blocks, B, LANES), F32),
            pltpu.VMEM((blocks, terms * B, LANES), BF16),
            pltpu.VMEM((STATS - 1, (blocks + 1) * 8, B), F32),
        ],
        compiler_params=params(24),
        name="image",
    )(slot, norm, received, lcomb, image, wave)
    stats = exchange(stats.reshape(peers, groups, LANES)).reshape(peers * groups, LANES)

    second, direction, projected = pl.pallas_call(
        functools.partial(second_kernel, float(blocks * peers * B * B)),
        out_shape=(of((blocks, B * B), F32), of((blocks, B * B), BF16), of((3,), F32)),
        in_specs=[VMEM] * 5,
        out_specs=(VMEM, VMEM, SMEM),
        scratch_shapes=[
            pltpu.VMEM((blocks * TILES + 8, LANES), F32),
            pltpu.VMEM((blocks * TILES + 8, LANES), F32),
            pltpu.VMEM((blocks, terms * B, LANES), BF16),
            pltpu.VMEM((blocks, B, B), BF16),
        ],
        compiler_params=params(24),
        name="second",
    )(stats, hpsi, wave, rsel, lcomb)
    return second, direction, projected


def solution(mesh):
    placed = (
        P(("parts", "sec"), None),
        P(("parts", "sec"), None, None),
        P(("parts", "sec"), None, None),
        P(("parts", "sec"), None, None),
        P(("parts", "sec")),
        P(("parts", "sec"), None),
        P(("parts", "sec")),
        P(("parts", "sec"), None),
    )
    return jax.shard_map(
        per_device,
        mesh=mesh,
        in_specs=placed,
        out_specs=(P(("parts", "sec"), None), P(("parts", "sec"), None), P("parts")),
        check_vma=False,
    )
```

```python
import functools

import jax
import jax.numpy as jnp
from jax import lax
from jax.experimental import pallas as pl
from jax.experimental.pallas import tpu as pltpu
from jax.sharding import PartitionSpec as P

B = 64
CAP = 2
LANES = 128
TILES = B * B // LANES
STATS = 5
SPACE = 16
TINY = 1e-30
ORDER = (11, 13, 15, 1, 2, 3, 7, 14, 6, 9, 5, 12, 8, 4, 10, 0)
SUM_ORDER = (11, 8, 14, 0, 9, 2, 6, 7, 5, 3, 12, 4, 1, 10, 13, 15)
F32 = jnp.float32
BF16 = jnp.bfloat16


def rounded_up(value, step):
    return -(-value // step) * step


def each(count, body):
    if count <= 32:
        for i in range(count):
            body(i)
    else:
        pl.loop(0, count)(body)


def run_of(peers):
    return 0 if peers % len(ORDER) else peers // len(ORDER)


def listed(peers, order):
    run = run_of(peers)
    return [q * run + i for q in order for i in range(run)] if run else list(range(peers))


def replaced(values, pairs, peers):
    run = run_of(peers)
    if not run:
        return values
    whole = values // run if run > 1 else values
    moved = values
    for old, new in pairs:
        moved = jnp.where(whole == old, values + (new - old) * run, moved)
    return moved


def dot(a, b):
    return jnp.dot(a, b, preferred_element_type=F32)


def summed(values):
    return jnp.sum(jnp.sum(values, axis=0, keepdims=True), axis=1, keepdims=True)


def low_half(rows=8):
    return lax.broadcasted_iota(jnp.int32, (rows, LANES), 1) < B


def swap(tile):
    return pltpu.roll(tile, B, 1)


def request_kernel(rsecs, owner, local, channel, table):
    terms, blocks = channel.shape
    peers = table.shape[0]
    peer = lax.broadcasted_iota(jnp.int32, (peers, LANES), 0)
    peer = replaced(peer, enumerate(ORDER), peers)
    lane = lax.broadcasted_iota(jnp.int32, (peers, LANES), 1)
    wanted = channel[...] * rsecs + local[...]
    seen = jnp.zeros((peers, LANES), jnp.int32)
    filled = jnp.zeros((peers, LANES), jnp.int32)
    for k in range(blocks):
        hit = peer == owner[:, k : k + 1]
        for j in range(terms):
            filled = jnp.where(hit & (lane == seen * terms + j), wanted[j : j + 1, k : k + 1], filled)
        seen = seen + hit.astype(jnp.int32)
    table[...] = filled[:, : table.shape[1]]


def gather_kernel(table, env, out):
    def fill(p):
        wanted = table[pl.ds(p, 1), :]
        for i in range(table.shape[1]):
            out[p, i * TILES : (i + 1) * TILES, :] = env[wanted[0, i]]

    each(out.shape[0], fill)


def prepare_kernel(
    peers, sector_far, owner_far, couple_far, psi_far, left_far, right_far, right, lcomb, image, wave, norm, slot,
    sector, owner, couple, psi, left_env, right_env, arrived, flat, right_stage, stage, twice,
):
    blocks, terms, chans = couple.shape
    lsecs = left_env.shape[1]
    rsecs = right_env.shape[1]
    wide = flat.shape[0]
    rows = blocks * terms
    moves = [
        pltpu.make_async_copy(source, target, arrived.at[i])
        for i, (source, target) in enumerate(
            (
                (right_far, right_env),
                (left_far, left_env),
                (psi_far, psi),
                (couple_far, couple),
                (sector_far, sector),
                (owner_far, owner),
            )
        )
    ]
    for move in moves:
        move.start()
    flat[chans * lsecs :, :] = jnp.zeros((wide - chans * lsecs, B * B), F32)
    moves[0].wait()

    for w in range(chans):
        slab = right_env[w].astype(F32)
        for t in range(TILES):
            right_stage[pl.ds(w * rsecs * TILES + t, rsecs, stride=TILES), :] = slab[:, t * LANES : (t + 1) * LANES]
    right[...] = right_stage[: chans * rsecs * TILES, :].reshape(right.shape).astype(BF16)

    for move in moves[1:]:
        move.wait()
    own = owner[...]
    lane = lax.broadcasted_iota(jnp.int32, own.shape, 1)
    rank = jnp.zeros_like(own)
    for k in range(blocks):
        rank = rank + ((own == own[:, k : k + 1]) & (lane > k)).astype(jnp.int32)
    slot[...] = replaced(own, [(peer, q) for q, peer in enumerate(ORDER)], peers) * CAP + rank

    is_low = low_half()

    for g in range(blocks // 8):
        waves = psi[g].astype(F32)
        for t in range(TILES):
            tile = waves[:, t * LANES : (t + 1) * LANES]
            base = 8 * g * B + t
            twice[pl.ds(base, 8, stride=B), :] = jnp.where(is_low, tile, swap(tile))
            twice[pl.ds(base + TILES, 8, stride=B), :] = jnp.where(is_low, swap(tile), tile)

    exact = jnp.concatenate([couple[:, j, :] for j in range(terms)], axis=0)
    high = exact.astype(BF16)
    rest = exact - high.astype(F32)
    middle = rest.astype(BF16)
    low = (rest - middle.astype(F32)).astype(BF16)
    column = lax.broadcasted_iota(jnp.int32, (chans, wide), 1)
    begin = lax.broadcasted_iota(jnp.int32, (chans, wide), 0) * lsecs
    spreads = ((column >= begin) & (column < begin + lsecs)).astype(F32).astype(BF16)
    wider = dot(jnp.concatenate([high, middle, low], axis=0), spreads)
    row = lax.broadcasted_iota(jnp.int32, (blocks, wide), 0)
    of_lane = lax.rem(lax.broadcasted_iota(jnp.int32, (blocks, wide), 1), lsecs)
    own_sector = sector[...]
    chosen = jnp.zeros((blocks, wide), jnp.int32)
    for k in range(blocks):
        chosen = jnp.where(row == k, own_sector[:, k : k + 1], chosen)
    mask = (chosen == of_lane).astype(F32)
    parts = (wider * jnp.concatenate([mask] * (3 * terms), axis=0)).astype(BF16)

    for w in range(chans):
        flat[w * lsecs : (w + 1) * lsecs, :] = left_env[w].astype(F32)
    width = 512
    for n in range(B * B // width):
        sums = dot(parts, flat[:, n * width : (n + 1) * width].astype(BF16))
        total = sums[:rows] + (sums[rows : 2 * rows] + sums[2 * rows :])
        for g in range(blocks // 8):
            for t in range(width // LANES):
                lanes = slice(t * LANES, (t + 1) * LANES)
                first = total[8 * g : 8 * g + 8, lanes]
                other = total[blocks + 8 * g : blocks + 8 * g + 8, lanes]
                base = 8 * g * B + n * (width // LANES) + t
                stage[pl.ds(base, 8, stride=B), :] = jnp.where(is_low, first, swap(other))
                stage[pl.ds(base + TILES, 8, stride=B), :] = jnp.where(is_low, swap(first), other)

    left_lanes = low_half(B)
    column = lax.broadcasted_iota(jnp.int32, (LANES, LANES), 0)
    within = column & (B - 1)
    moved = column - within + (within & 1) * TILES + (within >> 1)
    order = (lax.broadcasted_iota(jnp.int32, (LANES, LANES), 1) == moved).astype(F32).astype(BF16)

    def block(k):
        place = pl.ds(pl.multiple_of(k * B, B), B)
        left = dot(stage[place, :].astype(BF16), order).astype(BF16)
        base = twice[place, :]
        lcomb[k] = left
        wave[k] = base
        norm[pl.ds(k, 1), :] = summed(base[:, :B] * base[:, :B])
        both = jnp.concatenate([jnp.where(left_lanes, base, 0.0), jnp.where(left_lanes, 0.0, base)], axis=0)
        image[k] = dot(left, both.astype(BF16)).astype(BF16)

    each(blocks, block)


def fold(values):
    return jnp.sum(values[:, :B].reshape(B // 8, 8, B), axis=0)


def packed_rows(values):
    return jnp.where(low_half(TILES), values[:TILES], values[TILES:])


def image_kernel(slot, norm, received, lcomb, image, wave, hpsi, rsel, stats, stage, resid, zed, part):
    blocks = lcomb.shape[0]
    groups = blocks // 8
    places = slot[...]
    is_low = low_half(B)

    for k in range(blocks):
        raw = received[places[0, k]].astype(F32)
        turned = swap(raw)
        stage[pl.ds(k * 2 * B, B, stride=2), :] = jnp.where(is_low, raw, turned)
        stage[pl.ds(k * 2 * B + 1, B, stride=2), :] = jnp.where(is_low, turned, raw)

    def unfold(k):
        rsel[k] = stage[pl.ds(pl.multiple_of(k * 2 * B, 2 * B), 2 * B), :].astype(BF16)

    each(blocks, unfold)

    def keep(i, k, values):
        part[i, pl.ds(pl.multiple_of(k * 8, 8), 8), :] = fold(values)

    def of_group(i, g):
        sums = part[i, pl.ds(g * 8 * 8, 8, stride=8), :]
        for s in range(1, 8):
            sums = sums + part[i, pl.ds(g * 8 * 8 + s, 8, stride=8), :]
        return jnp.sum(sums, axis=1, keepdims=True)

    def apply(k):
        h = dot(image[k], rsel[k])
        hpsi[k] = h
        keep(0, k, wave[k] * h)

    each(blocks, apply)

    def group(g):
        own_norm, cross = norm[pl.ds(g * 8, 8), :], of_group(0, g)
        theta = cross / jnp.maximum(own_norm, TINY)

        for i in range(8):
            k = g * 8 + i
            h, base = hpsi[k], wave[k]
            rest = h - theta[i : i + 1, :] * base
            resid[k] = rest
            step = rest[:, :B].astype(BF16)
            zed[k, 0:B] = dot(step, rsel[k, 0:B]).astype(BF16)
            zed[k, B : 2 * B] = dot(step, rsel[k, B : 2 * B]).astype(BF16)
            keep(1, k, rest * rest)

        for i in range(8):
            k = g * 8 + i
            applied = dot(lcomb[k], zed[k])
            keep(2, k, resid[k] * applied)
            keep(3, k, wave[k] * applied)

        lane = lax.broadcasted_iota(jnp.int32, (8, LANES), 1)
        packed = jnp.zeros((8, LANES), F32)
        for i, value in enumerate([own_norm, cross] + [of_group(i, g) for i in range(1, STATS - 1)]):
            packed = jnp.where(lane == i, value, packed)
        spread = pltpu.roll(packed, 0, 1, stride=SPACE, stride_axis=0)
        row = jnp.sum(spread, axis=0, keepdims=True)
        if groups == 1:
            stats[...] = jnp.broadcast_to(row, stats.shape)
        else:
            pl.loop(0, stats.shape[0] // groups)(lambda p: stats.__setitem__((pl.ds(p * groups + g, 1), slice(None)), row))

    each(groups, group)


def second_kernel(count, stats, hpsi, wave, rsel, lcomb, second, direction, projected, stage, steps, zed, narrow):
    blocks = lcomb.shape[0]
    held = stats[...]
    here = lax.broadcasted_iota(jnp.int32, held.shape, 1) % SPACE == 0
    norm, cross, square, applied, crossed = (
        jnp.where(here, pltpu.roll(held, (LANES - i) % LANES, 1) if i else held, 0.0) for i in range(STATS)
    )

    theta = summed(cross) / summed(norm)
    own = cross / jnp.maximum(norm, TINY)
    mixed = cross - own * norm
    image = square + own * mixed
    shift = theta - own
    rr = summed(square - 2.0 * shift * mixed + shift * shift * norm)
    along = summed(applied - shift * (image + crossed) + shift * shift * cross)
    spread = rr / count
    scale = 1.0 / jnp.sqrt(spread + 1e-06)

    def rows_of(k):
        return pl.ds(k // 8 * (8 * TILES) + k % 8, TILES, stride=8)

    def move(k):
        step = ((hpsi[k] - theta * wave[k]) * scale).astype(BF16)
        narrow[k] = step[:, :B]
        steps[rows_of(k), :] = packed_rows(step.astype(F32))

    each(blocks, move)

    def apply(k):
        zed[k, 0:B] = dot(narrow[k], rsel[k, 0:B]).astype(BF16)
        zed[k, B : 2 * B] = dot(narrow[k], rsel[k, B : 2 * B]).astype(BF16)

    each(blocks, apply)

    def close(k):
        stage[rows_of(k), :] = packed_rows(dot(lcomb[k], zed[k]))

    each(blocks, close)

    def rows(g):
        place = pl.ds(pl.multiple_of(8 * g, 8), 8)
        for source, target in ((steps, direction), (stage, second)):
            for t in range(TILES):
                tile = source[pl.ds(pl.multiple_of((g * TILES + t) * 8, 8), 8), :]
                target[place, t * LANES : (t + 1) * LANES] = tile.astype(target.dtype)

    each(blocks // 8, rows)
    projected[0] = theta[0, 0]
    projected[1] = jnp.sqrt(spread)[0, 0]
    projected[2] = (along / rr)[0, 0]


VMEM = pl.BlockSpec(memory_space=pltpu.VMEM)
SMEM = pl.BlockSpec(memory_space=pltpu.SMEM)


def params(mib):
    return pltpu.CompilerParams(vmem_limit_bytes=mib << 20)


def cost(flops, moved):
    return pl.CostEstimate(flops=flops, bytes_accessed=moved, transcendentals=0)


def per_device(psi, left_env, right_env, couple, left_sector, right_owner, right_local, channel):
    peers = lax.axis_size("sec")
    blocks = psi.shape[0]
    _, terms, chans = couple.shape
    lsecs = left_env.shape[0]
    rsecs = right_env.shape[0]
    slots = peers * CAP
    groups = blocks // 8
    of = jax.ShapeDtypeStruct

    def exchange(values, order=ORDER):
        members = [listed(peers, order)]
        return lax.all_to_all(values, "sec", split_axis=0, concat_axis=0, axis_index_groups=members, tiled=True)

    owner = right_owner.T
    table = pl.pallas_call(
        functools.partial(request_kernel, rsecs),
        out_shape=of((peers, CAP * terms), jnp.int32),
        in_specs=[VMEM] * 3,
        out_specs=VMEM,
        compiler_params=params(4),
        cost_estimate=cost(0, 0),
        name="request",
    )(owner, right_local.reshape(1, blocks), channel.T)
    wanted = exchange(table.reshape(peers, 1, CAP * terms)).reshape(peers, CAP * terms)

    wide = rounded_up(lsecs * chans, LANES)
    inputs = (
        left_sector.reshape(1, blocks),
        owner,
        couple,
        psi.reshape(groups, 8, B * B),
        left_env.transpose(1, 0, 2),
        right_env.transpose(1, 0, 2),
    )
    right, lcomb, image, wave, norm, slot = pl.pallas_call(
        functools.partial(prepare_kernel, peers),
        out_shape=(
            of((chans * rsecs, TILES, LANES), BF16),
            of((blocks, B, terms * B), BF16),
            of((blocks, B, terms * B), BF16),
            of((blocks, B, LANES), F32),
            of((blocks, 1), F32),
            of((1, blocks), jnp.int32),
        ),
        in_specs=[pl.BlockSpec(memory_space=pl.ANY)] * len(inputs),
        out_specs=(VMEM,) * 6,
        scratch_shapes=[pltpu.VMEM(x.shape, x.dtype) for x in inputs]
        + [
            pltpu.SemaphoreType.DMA((len(inputs),)),
            pltpu.VMEM((wide, B * B), F32),
            pltpu.VMEM(((chans * rsecs + 1) * TILES, LANES), F32),
            pltpu.VMEM(((blocks + 1) * B, LANES), F32),
            pltpu.VMEM(((blocks + 1) * B, LANES), F32),
        ],
        compiler_params=params(24),
        cost_estimate=cost(100_000_000, 3_000_000),
        name="prepare",
    )(*[pltpu.with_memory_space_constraint(x, pltpu.HBM) for x in inputs])

    sent = pl.pallas_call(
        gather_kernel,
        out_shape=of((peers, CAP * terms * TILES, LANES), BF16),
        in_specs=[VMEM, VMEM],
        out_specs=VMEM,
        compiler_params=params(8),
        name="gather",
    )(wanted, right)
    received = exchange(sent).reshape(slots, terms * TILES, LANES)

    hpsi, rsel, stats = pl.pallas_call(
        image_kernel,
        out_shape=(
            of((blocks, B, LANES), F32),
            of((blocks, terms * B, LANES), BF16),
            of((peers * groups, LANES), F32),
        ),
        in_specs=[VMEM] * 6,
        out_specs=(VMEM, VMEM, VMEM),
        scratch_shapes=[
            pltpu.VMEM(((blocks * terms + 1) * B, LANES), F32),
            pltpu.VMEM((blocks, B, LANES), F32),
            pltpu.VMEM((blocks, terms * B, LANES), BF16),
            pltpu.VMEM((STATS - 1, (blocks + 1) * 8, B), F32),
        ],
        compiler_params=params(24),
        name="image",
    )(slot, norm, received, lcomb, image, wave)
    stats = exchange(stats.reshape(peers, groups, LANES), SUM_ORDER).reshape(peers * groups, LANES)

    second, direction, projected = pl.pallas_call(
        functools.partial(second_kernel, float(blocks * peers * B * B)),
        out_shape=(of((blocks, B * B), F32), of((blocks, B * B), BF16), of((3,), F32)),
        in_specs=[VMEM] * 5,
        out_specs=(VMEM, VMEM, SMEM),
        scratch_shapes=[
            pltpu.VMEM((blocks * TILES + 8, LANES), F32),
            pltpu.VMEM((blocks * TILES + 8, LANES), F32),
            pltpu.VMEM((blocks, terms * B, LANES), BF16),
            pltpu.VMEM((blocks, B, B), BF16),
        ],
        compiler_params=params(24),
        name="second",
    )(stats, hpsi, wave, rsel, lcomb)
    return second, direction, projected


def solution(mesh):
    placed = (
        P(("parts", "sec"), None),
        P(("parts", "sec"), None, None),
        P(("parts", "sec"), None, None),
        P(("parts", "sec"), None, None),
        P(("parts", "sec")),
        P(("parts", "sec"), None),
        P(("parts", "sec")),
        P(("parts", "sec"), None),
    )
    return jax.shard_map(
        per_device,
        mesh=mesh,
        in_specs=placed,
        out_specs=(P(("parts", "sec"), None), P(("parts", "sec"), None), P("parts")),
        check_vma=False,
    )
```

```python
import functools

import jax
import jax.numpy as jnp
from jax import lax
from jax.experimental import pallas as pl
from jax.experimental.pallas import tpu as pltpu
from jax.sharding import PartitionSpec as P

B = 64
CAP = 2
LANES = 128
TILES = B * B // LANES
STATS = 5
SPACE = 16
TINY = 1e-30
ORDER = (11, 13, 15, 1, 2, 3, 7, 14, 6, 9, 5, 12, 8, 4, 10, 0)
SUM_ORDER = (11, 8, 14, 0, 9, 2, 6, 7, 5, 3, 12, 4, 1, 10, 13, 15)
F32 = jnp.float32
BF16 = jnp.bfloat16


def rounded_up(value, step):
    return -(-value // step) * step


def each(count, body):
    if count <= 32:
        for i in range(count):
            body(i)
    else:
        pl.loop(0, count)(body)


def run_of(peers):
    return 0 if peers % len(ORDER) else peers // len(ORDER)


def listed(peers, order):
    run = run_of(peers)
    return [q * run + i for q in order for i in range(run)] if run else list(range(peers))


def replaced(values, pairs, peers):
    run = run_of(peers)
    if not run:
        return values
    whole = values // run if run > 1 else values
    moved = values
    for old, new in pairs:
        moved = jnp.where(whole == old, values + (new - old) * run, moved)
    return moved


def dot(a, b):
    return jnp.dot(a, b, preferred_element_type=F32)


def summed(values):
    return jnp.sum(jnp.sum(values, axis=0, keepdims=True), axis=1, keepdims=True)


def low_half(rows=8):
    return lax.broadcasted_iota(jnp.int32, (rows, LANES), 1) < B


def swap(tile):
    return pltpu.roll(tile, B, 1)


def request_kernel(rsecs, owner, local, channel, table):
    terms, blocks = channel.shape
    peers = table.shape[0]
    peer = lax.broadcasted_iota(jnp.int32, (peers, LANES), 0)
    peer = replaced(peer, enumerate(ORDER), peers)
    lane = lax.broadcasted_iota(jnp.int32, (peers, LANES), 1)
    wanted = channel[...] * rsecs + local[...]
    seen = jnp.zeros((peers, LANES), jnp.int32)
    filled = jnp.zeros((peers, LANES), jnp.int32)
    for k in range(blocks):
        hit = peer == owner[:, k : k + 1]
        for j in range(terms):
            filled = jnp.where(hit & (lane == seen * terms + j), wanted[j : j + 1, k : k + 1], filled)
        seen = seen + hit.astype(jnp.int32)
    table[...] = filled[:, : table.shape[1]]


def gather_kernel(table, env, out):
    def fill(p):
        wanted = table[pl.ds(p, 1), :]
        for i in range(table.shape[1]):
            out[p, i * TILES : (i + 1) * TILES, :] = env[wanted[0, i]]

    each(out.shape[0], fill)


def prepare_kernel(
    peers, sector_far, owner_far, couple_far, psi_far, left_far, right_far, right, lcomb, image, wave, norm, slot,
    sector, owner, couple, psi, left_env, right_env, arrived, flat, right_stage, stage, twice,
):
    blocks, terms, chans = couple.shape
    lsecs = left_env.shape[1]
    rsecs = right_env.shape[1]
    wide = flat.shape[0]
    rows = blocks * terms
    moves = [
        pltpu.make_async_copy(source, target, arrived.at[i])
        for i, (source, target) in enumerate(
            (
                (right_far, right_env),
                (left_far, left_env),
                (psi_far, psi),
                (couple_far, couple),
                (sector_far, sector),
                (owner_far, owner),
            )
        )
    ]
    for move in moves:
        move.start()
    flat[chans * lsecs :, :] = jnp.zeros((wide - chans * lsecs, B * B), F32)
    moves[0].wait()

    for w in range(chans):
        slab = right_env[w].astype(F32)
        for t in range(TILES):
            right_stage[pl.ds(w * rsecs * TILES + t, rsecs, stride=TILES), :] = slab[:, t * LANES : (t + 1) * LANES]
    right[...] = right_stage[: chans * rsecs * TILES, :].reshape(right.shape).astype(BF16)

    for move in moves[1:]:
        move.wait()
    own = owner[...]
    lane = lax.broadcasted_iota(jnp.int32, own.shape, 1)
    rank = jnp.zeros_like(own)
    for k in range(blocks):
        rank = rank + ((own == own[:, k : k + 1]) & (lane > k)).astype(jnp.int32)
    slot[...] = replaced(own, [(peer, q) for q, peer in enumerate(ORDER)], peers) * CAP + rank

    is_low = low_half()

    for g in range(blocks // 8):
        waves = psi[g].astype(F32)
        for t in range(TILES):
            tile = waves[:, t * LANES : (t + 1) * LANES]
            base = 8 * g * B + t
            twice[pl.ds(base, 8, stride=B), :] = jnp.where(is_low, tile, swap(tile))
            twice[pl.ds(base + TILES, 8, stride=B), :] = jnp.where(is_low, swap(tile), tile)

    exact = jnp.concatenate([couple[:, j, :] for j in range(terms)], axis=0)
    high = exact.astype(BF16)
    rest = exact - high.astype(F32)
    middle = rest.astype(BF16)
    low = (rest - middle.astype(F32)).astype(BF16)
    column = lax.broadcasted_iota(jnp.int32, (chans, wide), 1)
    begin = lax.broadcasted_iota(jnp.int32, (chans, wide), 0) * lsecs
    spreads = ((column >= begin) & (column < begin + lsecs)).astype(F32).astype(BF16)
    wider = dot(jnp.concatenate([high, middle, low], axis=0), spreads)
    row = lax.broadcasted_iota(jnp.int32, (blocks, wide), 0)
    of_lane = lax.rem(lax.broadcasted_iota(jnp.int32, (blocks, wide), 1), lsecs)
    own_sector = sector[...]
    chosen = jnp.zeros((blocks, wide), jnp.int32)
    for k in range(blocks):
        chosen = jnp.where(row == k, own_sector[:, k : k + 1], chosen)
    mask = (chosen == of_lane).astype(F32)
    parts = (wider * jnp.concatenate([mask] * (3 * terms), axis=0)).astype(BF16)

    for w in range(chans):
        flat[w * lsecs : (w + 1) * lsecs, :] = left_env[w].astype(F32)
    width = 512
    for n in range(B * B // width):
        sums = dot(parts, flat[:, n * width : (n + 1) * width].astype(BF16))
        total = sums[:rows] + (sums[rows : 2 * rows] + sums[2 * rows :])
        for g in range(blocks // 8):
            for t in range(width // LANES):
                lanes = slice(t * LANES, (t + 1) * LANES)
                first = total[8 * g : 8 * g + 8, lanes]
                other = total[blocks + 8 * g : blocks + 8 * g + 8, lanes]
                base = 8 * g * B + n * (width // LANES) + t
                stage[pl.ds(base, 8, stride=B), :] = jnp.where(is_low, first, swap(other))
                stage[pl.ds(base + TILES, 8, stride=B), :] = jnp.where(is_low, swap(first), other)

    left_lanes = low_half(B)
    column = lax.broadcasted_iota(jnp.int32, (LANES, LANES), 0)
    within = column & (B - 1)
    moved = column - within + (within & 1) * TILES + (within >> 1)
    order = (lax.broadcasted_iota(jnp.int32, (LANES, LANES), 1) == moved).astype(F32).astype(BF16)

    def block(k):
        place = pl.ds(pl.multiple_of(k * B, B), B)
        left = dot(stage[place, :].astype(BF16), order).astype(BF16)
        base = twice[place, :]
        lcomb[k] = left
        wave[k] = base
        norm[pl.ds(k, 1), :] = summed(base[:, :B] * base[:, :B])
        both = jnp.concatenate([jnp.where(left_lanes, base, 0.0), jnp.where(left_lanes, 0.0, base)], axis=0)
        image[k] = dot(left, both.astype(BF16)).astype(BF16)

    each(blocks, block)


def fold(values):
    return jnp.sum(values[:, :B].reshape(B // 8, 8, B), axis=0)


def packed_rows(values):
    return jnp.where(low_half(TILES), values[:TILES], values[TILES:])


def image_kernel(slot, norm, received, lcomb, image, wave, hpsi, rsel, stats, stage, resid, zed, part):
    blocks = lcomb.shape[0]
    groups = blocks // 8
    places = slot[...]
    is_low = low_half(B)

    for k in range(blocks):
        raw = received[places[0, k]].astype(F32)
        turned = swap(raw)
        stage[pl.ds(k * 2 * B, B, stride=2), :] = jnp.where(is_low, raw, turned)
        stage[pl.ds(k * 2 * B + 1, B, stride=2), :] = jnp.where(is_low, turned, raw)

    def unfold(k):
        rsel[k] = stage[pl.ds(pl.multiple_of(k * 2 * B, 2 * B), 2 * B), :].astype(BF16)

    each(blocks, unfold)

    def keep(i, k, values):
        part[i, pl.ds(pl.multiple_of(k * 8, 8), 8), :] = fold(values)

    def of_group(i, g):
        sums = part[i, pl.ds(g * 8 * 8, 8, stride=8), :]
        for s in range(1, 8):
            sums = sums + part[i, pl.ds(g * 8 * 8 + s, 8, stride=8), :]
        return jnp.sum(sums, axis=1, keepdims=True)

    def apply(k):
        h = dot(image[k], rsel[k])
        hpsi[k] = h
        keep(0, k, wave[k] * h)

    each(blocks, apply)

    def group(g):
        own_norm, cross = norm[pl.ds(g * 8, 8), :], of_group(0, g)
        theta = cross / jnp.maximum(own_norm, TINY)

        for i in range(8):
            k = g * 8 + i
            h, base = hpsi[k], wave[k]
            rest = h - theta[i : i + 1, :] * base
            resid[k] = rest
            step = rest[:, :B].astype(BF16)
            zed[k, 0:B] = dot(step, rsel[k, 0:B]).astype(BF16)
            zed[k, B : 2 * B] = dot(step, rsel[k, B : 2 * B]).astype(BF16)
            keep(1, k, rest * rest)

        for i in range(8):
            k = g * 8 + i
            applied = dot(lcomb[k], zed[k])
            keep(2, k, resid[k] * applied)
            keep(3, k, wave[k] * applied)

        lane = lax.broadcasted_iota(jnp.int32, (8, LANES), 1)
        packed = jnp.zeros((8, LANES), F32)
        for i, value in enumerate([own_norm, cross] + [of_group(i, g) for i in range(1, STATS - 1)]):
            packed = jnp.where(lane == i, value, packed)
        spread = pltpu.roll(packed, 0, 1, stride=SPACE, stride_axis=0)
        row = jnp.sum(spread, axis=0, keepdims=True)
        if groups == 1:
            stats[...] = jnp.broadcast_to(row, stats.shape)
        else:
            pl.loop(0, stats.shape[0] // groups)(lambda p: stats.__setitem__((pl.ds(p * groups + g, 1), slice(None)), row))

    each(groups, group)


def second_kernel(count, stats, hpsi, wave, rsel, lcomb, second, direction, projected, stage, steps, zed, narrow):
    blocks = lcomb.shape[0]
    held = stats[...]
    here = lax.broadcasted_iota(jnp.int32, held.shape, 1) % SPACE == 0
    norm, cross, square, applied, crossed = (
        jnp.where(here, pltpu.roll(held, (LANES - i) % LANES, 1) if i else held, 0.0) for i in range(STATS)
    )

    theta = summed(cross) / summed(norm)
    own = cross / jnp.maximum(norm, TINY)
    mixed = cross - own * norm
    image = square + own * mixed
    shift = theta - own
    rr = summed(square - 2.0 * shift * mixed + shift * shift * norm)
    along = summed(applied - shift * (image + crossed) + shift * shift * cross)
    spread = rr / count
    scale = 1.0 / jnp.sqrt(spread + 1e-06)

    def rows_of(k):
        return pl.ds(k // 8 * (8 * TILES) + k % 8, TILES, stride=8)

    def move(k):
        step = ((hpsi[k] - theta * wave[k]) * scale).astype(BF16)
        narrow[k] = step[:, :B]
        steps[rows_of(k), :] = packed_rows(step.astype(F32))

    each(blocks, move)

    def rows(source, target, g):
        place = pl.ds(pl.multiple_of(8 * g, 8), 8)
        for t in range(TILES):
            tile = source[pl.ds(pl.multiple_of((g * TILES + t) * 8, 8), 8), :]
            target[place, t * LANES : (t + 1) * LANES] = tile.astype(target.dtype)

    each(blocks // 8, functools.partial(rows, steps, direction))

    def apply(k):
        zed[k, 0:B] = dot(narrow[k], rsel[k, 0:B]).astype(BF16)
        zed[k, B : 2 * B] = dot(narrow[k], rsel[k, B : 2 * B]).astype(BF16)

    each(blocks, apply)

    def close(k):
        stage[rows_of(k), :] = packed_rows(dot(lcomb[k], zed[k]))

    each(blocks, close)

    each(blocks // 8, functools.partial(rows, stage, second))
    projected[0] = theta[0, 0]
    projected[1] = jnp.sqrt(spread)[0, 0]
    projected[2] = (along / rr)[0, 0]


VMEM = pl.BlockSpec(memory_space=pltpu.VMEM)
SMEM = pl.BlockSpec(memory_space=pltpu.SMEM)


def params(mib):
    return pltpu.CompilerParams(vmem_limit_bytes=mib << 20)


def cost(flops, moved):
    return pl.CostEstimate(flops=flops, bytes_accessed=moved, transcendentals=0)


def per_device(psi, left_env, right_env, couple, left_sector, right_owner, right_local, channel):
    peers = lax.axis_size("sec")
    blocks = psi.shape[0]
    _, terms, chans = couple.shape
    lsecs = left_env.shape[0]
    rsecs = right_env.shape[0]
    slots = peers * CAP
    groups = blocks // 8
    of = jax.ShapeDtypeStruct

    def exchange(values, order=ORDER):
        members = [listed(peers, order)]
        return lax.all_to_all(values, "sec", split_axis=0, concat_axis=0, axis_index_groups=members, tiled=True)

    owner = right_owner.T
    table = pl.pallas_call(
        functools.partial(request_kernel, rsecs),
        out_shape=of((peers, CAP * terms), jnp.int32),
        in_specs=[VMEM] * 3,
        out_specs=VMEM,
        compiler_params=params(4),
        cost_estimate=cost(0, 0),
        name="request",
    )(owner, right_local.reshape(1, blocks), channel.T)
    wanted = exchange(table.reshape(peers, 1, CAP * terms)).reshape(peers, CAP * terms)

    wide = rounded_up(lsecs * chans, LANES)
    inputs = (
        left_sector.reshape(1, blocks),
        owner,
        couple,
        psi.reshape(groups, 8, B * B),
        left_env.transpose(1, 0, 2),
        right_env.transpose(1, 0, 2),
    )
    right, lcomb, image, wave, norm, slot = pl.pallas_call(
        functools.partial(prepare_kernel, peers),
        out_shape=(
            of((chans * rsecs, TILES, LANES), BF16),
            of((blocks, B, terms * B), BF16),
            of((blocks, B, terms * B), BF16),
            of((blocks, B, LANES), F32),
            of((blocks, 1), F32),
            of((1, blocks), jnp.int32),
        ),
        in_specs=[pl.BlockSpec(memory_space=pl.ANY)] * len(inputs),
        out_specs=(VMEM,) * 6,
        scratch_shapes=[pltpu.VMEM(x.shape, x.dtype) for x in inputs]
        + [
            pltpu.SemaphoreType.DMA((len(inputs),)),
            pltpu.VMEM((wide, B * B), F32),
            pltpu.VMEM(((chans * rsecs + 1) * TILES, LANES), F32),
            pltpu.VMEM(((blocks + 1) * B, LANES), F32),
            pltpu.VMEM(((blocks + 1) * B, LANES), F32),
        ],
        compiler_params=params(24),
        cost_estimate=cost(100_000_000, 3_000_000),
        name="prepare",
    )(*[pltpu.with_memory_space_constraint(x, pltpu.HBM) for x in inputs])

    sent = pl.pallas_call(
        gather_kernel,
        out_shape=of((peers, CAP * terms * TILES, LANES), BF16),
        in_specs=[VMEM, VMEM],
        out_specs=VMEM,
        compiler_params=params(8),
        name="gather",
    )(wanted, right)
    received = exchange(sent).reshape(slots, terms * TILES, LANES)

    hpsi, rsel, stats = pl.pallas_call(
        image_kernel,
        out_shape=(
            of((blocks, B, LANES), F32),
            of((blocks, terms * B, LANES), BF16),
            of((peers * groups, LANES), F32),
        ),
        in_specs=[VMEM] * 6,
        out_specs=(VMEM, VMEM, VMEM),
        scratch_shapes=[
            pltpu.VMEM(((blocks * terms + 1) * B, LANES), F32),
            pltpu.VMEM((blocks, B, LANES), F32),
            pltpu.VMEM((blocks, terms * B, LANES), BF16),
            pltpu.VMEM((STATS - 1, (blocks + 1) * 8, B), F32),
        ],
        compiler_params=params(24),
        name="image",
    )(slot, norm, received, lcomb, image, wave)
    stats = exchange(stats.reshape(peers, groups, LANES), SUM_ORDER).reshape(peers * groups, LANES)

    second, direction, projected = pl.pallas_call(
        functools.partial(second_kernel, float(blocks * peers * B * B)),
        out_shape=(of((blocks, B * B), F32), of((blocks, B * B), BF16), of((3,), F32)),
        in_specs=[VMEM] * 5,
        out_specs=(VMEM, VMEM, SMEM),
        scratch_shapes=[
            pltpu.VMEM((blocks * TILES + 8, LANES), F32),
            pltpu.VMEM((blocks * TILES + 8, LANES), F32),
            pltpu.VMEM((blocks, terms * B, LANES), BF16),
            pltpu.VMEM((blocks, B, B), BF16),
        ],
        compiler_params=params(24),
        name="second",
    )(stats, hpsi, wave, rsel, lcomb)
    return second, direction, projected


def solution(mesh):
    placed = (
        P(("parts", "sec"), None),
        P(("parts", "sec"), None, None),
        P(("parts", "sec"), None, None),
        P(("parts", "sec"), None, None),
        P(("parts", "sec")),
        P(("parts", "sec"), None),
        P(("parts", "sec")),
        P(("parts", "sec"), None),
    )
    return jax.shard_map(
        per_device,
        mesh=mesh,
        in_specs=placed,
        out_specs=(P(("parts", "sec"), None), P(("parts", "sec"), None), P("parts")),
        check_vma=False,
    )
```
